32 devices in a mesh: row: 4 (over y, x), col: 4 (over z), layer: 2 (over core).
Axes of the slice: x: 2, y: 2, z: 4, core: 2. Of those that a mesh axis runs over, the one named last changes fastest.
Arguments:
- a_blocks: bfloat16 [4, 4, 2, 16, 2, 128, 128], P('row', 'col', 'layer'), may hold values from -6 to 6
- a_cols: int32 [4, 4, 2, 16, 2], P('row', 'col', 'layer'), may hold values from 0 to 47, as said below
- a_count: int32 [4, 4, 2, 16], P('row', 'col', 'layer'), may hold values from 1 to 2
- b_blocks: bfloat16 [4, 4, 2, 48, 2, 128, 128], P('row', 'col', 'layer'), may hold values from -0.5 to 0.5
- b_cols: int32 [4, 4, 2, 48, 2], P('row', 'col', 'layer'), may hold values from 0 to 47, as said below
- b_count: int32 [4, 4, 2, 48], P('row', 'col', 'layer'), may hold values from 1 to 2
- c_cols: int32 [4, 4, 16, 2], P('row', 'col'), may hold values from 0 to 47, as said below
Outputs:
- c_blocks: bfloat16 [4, 4, 16, 2, 128, 128], P('row', 'col', 'layer')
The draws below stay inside these ranges and needn't reach their ends.
Inputs may be any that keep to these rules, and one draw needn't show every extreme that they name: a_cols of block row r is one of 3 * r - 1, 3 * r, 3 * r + 1 modulo 48; the slots of one block row are distinct. b_cols of block row m is one of m - 1, m, m + 1 modulo 48; the slots of one block row are distinct. c_cols of block row r is one of 3 * r - 1, 3 * r, 3 * r + 1 modulo 48; the slots of one block row are distinct.
All inputs are finite; a program needn't handle non-finite values.
Results may differ from the reference program's by a relative error of at most 0.001.
Values may be sent and summed in bfloat16 or wider, within the bound.
A program may use at most 64 MiB of HBM per device.

```python
import jax
import jax.numpy as jnp
from jax import lax

BS = 128
PB = 48
PR = 16
KA = 2
KB = 2
KC = 2
STEPS = 2
STRIDE = 3
N_ROW = 4
N_COL = 4
N_LAYER = 2


def band_offsets(key, extent):
    last = len(extent) - 1
    first_offset = jax.random.randint(jax.random.fold_in(key, 1), extent[:-1] + (1,), 0, 3)
    offset_step = jax.random.randint(jax.random.fold_in(key, 2), extent[:-1] + (1,), 1, 3)
    slot_index = lax.broadcasted_iota(jnp.int32, extent, last)
    return (first_offset + slot_index * offset_step) % 3 - 1


def draw_a_cols(key, part):
    key = jax.random.fold_in(key, 11)
    extent = (N_ROW, N_COL, N_LAYER, PR, KA)
    centre = lax.broadcasted_iota(jnp.int32, extent, 3) * STRIDE
    return ((centre + band_offsets(key, extent)) % PB).astype(jnp.int32)


def draw_b_cols(key, part):
    key = jax.random.fold_in(key, 23)
    extent = (N_ROW, N_COL, N_LAYER, PB, KB)
    centre = lax.broadcasted_iota(jnp.int32, extent, 3)
    return ((centre + band_offsets(key, extent)) % PB).astype(jnp.int32)


def draw_c_cols(key, part):
    key = jax.random.fold_in(key, 37)
    extent = (N_ROW, N_COL, PR, KC)
    centre = lax.broadcasted_iota(jnp.int32, extent, 2) * STRIDE
    return ((centre + band_offsets(key, extent)) % PB).astype(jnp.int32)


def plant(result, key, least, high):
    dims = result.shape
    spot = [jax.random.randint(jax.random.fold_in(key, axis), (), 0, dims[axis]) for axis in range(len(dims))]
    result = result.at[tuple(spot)].set(least)
    longest = dims.index(max(dims))
    spot[longest] = (spot[longest] + 1) % dims[longest]
    return result.at[tuple(spot)].set(high)


def block_scale(own_key, shape, pieces, smallest, largest):
    def one(dim, parts):
        steps = jax.random.uniform(jax.random.fold_in(jax.random.fold_in(own_key, 6), dim), (parts,), jnp.float32, smallest / len(pieces), largest / len(pieces))
        return jnp.repeat(jnp.exp(steps), shape[dim] // parts).reshape((-1,) + (1,) * (len(shape) - dim - 1))

    level = one(*pieces[0])
    for cut in pieces[1:]:
        level = level * one(*cut)
    return level


def noise(own_key, shape, width, limit, shards=(), kind=jnp.bfloat16):
    level = block_scale(own_key, shape, shards, -0.22, 0.18) if shards else 1.0
    values = jax.random.normal(own_key, shape, jnp.float32) * width * level
    return jnp.minimum(jnp.maximum(values, -limit), limit).astype(kind)


def setup_inputs(seed: int = 0) -> dict:
    splits = jax.random.split(jax.random.key(seed), 8)
    a_blocks = noise(splits[0], (N_ROW, N_COL, N_LAYER, PR, KA, BS, BS), 1.0, 6.0, ((0, 4), (1, 4), (2, 2)))
    a_cols = draw_a_cols(jax.random.fold_in(splits[7], 71), 0)
    a_count = plant(jax.random.randint(splits[2], (N_ROW, N_COL, N_LAYER, PR), 1, KA + 1), jax.random.fold_in(splits[2], 1), 1, KA).astype(jnp.int32)
    b_blocks = noise(splits[3], (N_ROW, N_COL, N_LAYER, PB, KB, BS, BS), BS ** -0.5, 0.5, ((0, 4), (1, 4), (2, 2)))
    b_cols = draw_b_cols(jax.random.fold_in(splits[7], 71), 0)
    b_count = plant(jax.random.randint(splits[5], (N_ROW, N_COL, N_LAYER, PB), 1, KB + 1), jax.random.fold_in(splits[5], 1), 1, KB).astype(jnp.int32)
    c_cols = draw_c_cols(jax.random.fold_in(splits[7], 71), 0)
    return dict(a_blocks=a_blocks, a_cols=a_cols, a_count=a_count, b_blocks=b_blocks, b_cols=b_cols, b_count=b_count, c_cols=c_cols)


def panel_product(a_panel, a_index, a_live, b_panel, b_index, b_live, out_cols):
    chosen = jnp.take(b_panel, a_index, axis=0).astype(jnp.float32)
    chosen_cols = jnp.take(b_index, a_index, axis=0)
    chosen_live = jnp.take(b_live, a_index, axis=0)
    slot_a = lax.broadcasted_iota(jnp.int32, chosen_cols.shape, 1)
    slot_b = lax.broadcasted_iota(jnp.int32, chosen_cols.shape, 2)
    usable = (slot_a < a_live[:, None, None]) & (slot_b < chosen_live[:, :, None])
    matches = (chosen_cols[:, :, :, None] == out_cols[:, None, None, :]) & usable[:, :, :, None]
    products = jnp.einsum("rtxy,rtuyz->rtuxz", a_panel.astype(jnp.float32), chosen,
                          precision=lax.Precision.HIGHEST)
    return jnp.einsum("rtuv,rtuxz->rvxz", matches.astype(jnp.float32), products,
                      precision=lax.Precision.HIGHEST)


def reference(a_blocks, a_cols, a_count, b_blocks, b_cols, b_count, c_cols):
    def row_terms(row_index):
        a_row = a_blocks[row_index]
        a_row_cols = a_cols[row_index]
        a_row_live = a_count[row_index]
        out_row = c_cols[row_index]
        accumulated = jnp.zeros((N_COL, PR, KC, BS, BS), jnp.float32)
        for cannon_step in range(STEPS):
            source = (row_index + cannon_step) % N_ROW
            b_row = b_blocks[source]
            b_row_cols = b_cols[source]
            b_row_live = b_count[source]
            for layer_index in range(N_LAYER):
                a_panels = jnp.roll(a_row[:, layer_index], -cannon_step, axis=0)
                a_lists = jnp.roll(a_row_cols[:, layer_index], -cannon_step, axis=0)
                a_lives = jnp.roll(a_row_live[:, layer_index], -cannon_step, axis=0)
                accumulated = accumulated + jax.vmap(panel_product)(
                    a_panels, a_lists, a_lives,
                    b_row[:, layer_index], b_row_cols[:, layer_index], b_row_live[:, layer_index],
                    out_row)
        return accumulated.astype(jnp.bfloat16)

    return lax.map(row_terms, jnp.arange(N_ROW, dtype=jnp.int32))
```

```python
import functools

import jax
import jax.numpy as jnp
from jax import lax
from jax.experimental import pallas as pl
from jax.experimental.pallas import tpu as pltpu
from jax.sharding import PartitionSpec as P

STEPS = 2
CAPACITY = 32
CHUNKS = 4
ABSENT = 1000
LANES = 128


def passed_along(value, axis, steps):
    count = lax.axis_size(axis)
    pairs = [(source, (source + steps) % count) for source in range(count)]
    return lax.ppermute(value, axis, pairs)


def pick_rows(panel, index, live, wanted):
    return (
        jnp.take(panel, wanted, axis=0),
        jnp.take(index, wanted, axis=0),
        jnp.take(live, wanted, axis=0),
    )


def panel_terms(a_panel, a_live, chosen, chosen_cols, chosen_live, out_cols):
    slot_a = lax.broadcasted_iota(jnp.int32, chosen_cols.shape, 1)
    slot_b = lax.broadcasted_iota(jnp.int32, chosen_cols.shape, 2)
    usable = (slot_a < a_live[:, None, None]) & (slot_b < chosen_live[:, :, None])
    matches = (chosen_cols[:, :, :, None] == out_cols[:, None, None, :]) & usable[:, :, :, None]
    products = jnp.einsum("rtxy,rtuyz->rtuxz", a_panel, chosen, preferred_element_type=jnp.float32)
    return jnp.einsum(
        "rtuv,rtuxz->rvxz", matches.astype(jnp.float32), products, precision=lax.Precision.HIGHEST
    )


def general(a_panel, a_index, a_live, b_panel, b_index, b_live, out_cols):
    partial_value = jnp.zeros(
        (out_cols.shape[0], out_cols.shape[1], a_panel.shape[2], b_panel.shape[3]), jnp.float32
    )
    for cannon_step in range(STEPS):
        if cannon_step > 0:
            a_panel, a_index, a_live = passed_along((a_panel, a_index, a_live), "col", -1)
            b_panel, b_index, b_live = passed_along((b_panel, b_index, b_live), "row", -1)
        chosen, chosen_cols, chosen_live = pick_rows(b_panel, b_index, b_live, a_index)
        partial_value = partial_value + panel_terms(
            a_panel, a_live, chosen, chosen_cols, chosen_live, out_cols
        )
    summed = lax.psum_scatter(partial_value, "layer", scatter_dimension=0, tiled=True)
    return summed.astype(jnp.bfloat16)


def lists_of(a_cols, a_count, b_cols, b_count, c_cols):
    rows, ka = a_cols.shape
    kc = c_cols.shape[1]
    panel, kb = b_cols.shape
    stride = panel // rows
    r = lax.broadcasted_iota(jnp.int32, (rows, ka), 0)
    t = lax.broadcasted_iota(jnp.int32, (rows, ka), 1)
    offset = (a_cols - stride * r + 1 + panel) % panel
    offset = jnp.where(t < a_count[:, None], offset, ABSENT)
    u = lax.broadcasted_iota(jnp.int32, (panel, kb), 1)
    held = jnp.where(u < b_count[:, None], b_cols, -1)
    near = jnp.roll(held, 1, axis=0).reshape(rows, stride * kb)
    full = (rows, ka, kc)
    parts = [jnp.broadcast_to(offset[:, :, None], full), jnp.broadcast_to(c_cols[:, None, :], full)]
    parts += [jnp.broadcast_to(near[:, k, None, None], full) for k in range(stride * kb)]
    tile = jnp.stack([part.reshape(-1) for part in parts])
    return jnp.pad(tile, ((0, 0), (0, LANES - tile.shape[1])), constant_values=ABSENT)


def matched(a_row, c_row, b_rows, rows, panel, kb):
    shape = (8, LANES)
    stride = panel // rows
    lane = lax.broadcasted_iota(jnp.int32, shape, 1)
    r = lane // 4
    a_row = jnp.broadcast_to(a_row, shape)
    c_row = jnp.broadcast_to(c_row, shape)
    need = jnp.zeros(shape, jnp.int32)
    place = jnp.full(shape, panel * kb, jnp.int32)
    for d in range(stride):
        m = r * stride + (d - 1)
        m = jnp.where(m < 0, m + panel, m)
        for u in range(kb):
            k = d * kb + u
            hit = (a_row == d) & (c_row == jnp.broadcast_to(b_rows[k : k + 1], shape))
            hit = hit & (lane < rows * 4)
            need = jnp.where(hit, 1, need)
            place = jnp.where(hit, m * kb + u, place)
    return need, place


def earlier(need):
    lane = lax.broadcasted_iota(jnp.int32, need.shape, 1)
    total = need
    step = 1
    while step < LANES:
        total = total + jnp.where(lane >= step, pltpu.roll(total, step, 1), 0)
        step *= 2
    return total - need


def kernel(
    n_row, n_col, panel, kb,
    lists_ref, a_hbm, b_hbm,
    out_ref, flag_ref,
    av, bv, a_in, b_in, packed, part, layer_in, tiles, table_v, table_s, send_v, send_s,
    flag_own, flag_layer, flag_row_src, flag_row, flag_col_src, flag_col,
    local_sem, list_send, list_recv, a_send, a_recv, b_send, b_recv, l_send, l_recv,
    f0_send, f0_recv, f1_send, f1_recv, f2_send, f2_recv,
):
    row = lax.axis_index("row")
    col = lax.axis_index("col")
    layer = lax.axis_index("layer")
    rows = out_ref.shape[0] * 2
    half = rows // 2

    def at(d_row, d_col, d_layer=0):
        return {
            "row": lax.rem(row + d_row + n_row, n_row),
            "col": lax.rem(col + d_col + n_col, n_col),
            "layer": lax.rem(layer + d_layer, 2),
        }

    load_b = pltpu.make_async_copy(b_hbm, bv.at[pl.ds(0, panel * kb)], local_sem.at[0])
    load_b.start()
    load_a = pltpu.make_async_copy(a_hbm, av, local_sem.at[1])
    load_a.start()

    barrier = pltpu.get_barrier_semaphore()
    partners = [at(o, 0) for o in range(1, n_row)] + [at(0, o) for o in range(1, n_col)]
    partners += [at(0, 0, 1), at(1, -1), at(-1, 1)]
    for partner in partners:
        pl.semaphore_signal(barrier, inc=1, device_id=partner, device_id_type=pl.DeviceIdType.MESH)

    zero = jnp.zeros(bv.shape[1:], bv.dtype)
    bv[panel * kb] = zero
    b_in[CAPACITY] = zero
    own = lists_ref[...]
    need, place = matched(own[0:1], own[1:2], own[2:], rows, panel, kb)
    table_v[0] = place

    pl.semaphore_wait(barrier, len(partners))

    def remote(src, dst, send, recv, device):
        copy = pltpu.make_async_remote_copy(
            src_ref=src, dst_ref=dst, send_sem=send, recv_sem=recv,
            device_id=device, device_id_type=pl.DeviceIdType.MESH,
        )
        copy.start()
        return copy

    sends = {}
    for slot, device in ((2, at(1, 0)), (3, at(1, -1)), (1, at(-1, 0)), (0, at(0, -1))):
        sends[slot] = remote(lists_ref, tiles.at[slot], list_send.at[slot], list_recv.at[slot], device)
    a_copies = []
    per = av.shape[0] // CHUNKS
    for c in range(CHUNKS):
        piece = pl.ds(c * per, per)
        a_copies.append(
            remote(a_hbm.at[piece], a_in.at[piece], a_send.at[c], a_recv.at[c], at(0, -1))
        )

    sends[2].wait_recv()
    sends[3].wait_recv()
    need, place = matched(tiles[3, 0:1], tiles[2, 1:2], own[2:], rows, panel, kb)
    before = earlier(need)
    wanted = lax.broadcasted_iota(jnp.int32, (CAPACITY, LANES), 0)
    spread = (CAPACITY, LANES)
    here = (jnp.broadcast_to(before[0:1], spread) == wanted) & (
        jnp.broadcast_to(need[0:1], spread) > 0
    )
    chosen = jnp.sum(jnp.where(here, jnp.broadcast_to(place[0:1], spread), 0), axis=1, keepdims=True)
    send_v[...] = jnp.broadcast_to(chosen, spread)
    to_smem = pltpu.make_async_copy(send_v, send_s, local_sem.at[2])
    to_smem.start()
    lane = lax.broadcasted_iota(jnp.int32, (8, LANES), 1)
    last = jnp.where(lane == LANES - 1, before + need, 0)
    flag_own[...] = jnp.broadcast_to(jnp.max(last, axis=1, keepdims=True), (8, LANES))
    load_b.wait()
    to_smem.wait()
    b_copies = []
    per = CAPACITY // CHUNKS
    for c in range(CHUNKS):
        for k in range(c * per, (c + 1) * per):
            packed[k] = bv[send_s[k, 0]]
        piece = pl.ds(c * per, per)
        b_copies.append(
            remote(packed.at[piece], b_in.at[piece], b_send.at[c], b_recv.at[c], at(-1, 0))
        )
    f0 = remote(flag_own, flag_layer, f0_send.at[0], f0_recv.at[0], at(0, 0, 1))

    sends[0].wait_recv()
    sends[1].wait_recv()
    need, place = matched(tiles[0, 0:1], own[1:2], tiles[1][2:], rows, panel, kb)
    before = earlier(need)
    table_v[1] = jnp.where((need > 0) & (before < CAPACITY), before, CAPACITY)
    to_smem = pltpu.make_async_copy(table_v, table_s, local_sem.at[3])
    to_smem.start()

    f0.wait()
    flag_row_src[...] = jnp.maximum(flag_own[...], flag_layer[...])
    f1 = [
        remote(flag_row_src, flag_row.at[o - 1], f1_send.at[o - 1], f1_recv.at[o - 1], at(o, 0))
        for o in range(1, n_row)
    ]
    to_smem.wait()
    load_a.wait()

    def product(step, a, b, r):
        block = [b[table_s[step, 0, 4 * r + k]] for k in range(4)]
        left = jnp.concatenate([a[2 * r], a[2 * r + 1]], axis=1)
        right = jnp.concatenate(
            [jnp.concatenate(block[:2], axis=1), jnp.concatenate(block[2:], axis=1)], axis=0
        )
        return jnp.dot(left, right, preferred_element_type=jnp.float32)

    @pl.loop(0, rows, unroll=4)
    def _(r):
        part[r] = product(0, av, bv, r)

    worst = flag_row_src[...]
    for o in range(1, n_row):
        f1[o - 1].wait()
        worst = jnp.maximum(worst, flag_row[o - 1])
    flag_col_src[...] = worst
    f2 = [
        remote(flag_col_src, flag_col.at[o - 1], f2_send.at[o - 1], f2_recv.at[o - 1], at(0, o))
        for o in range(1, n_col)
    ]
    for o in range(1, n_col):
        f2[o - 1].wait()
        worst = jnp.maximum(worst, flag_col[o - 1])
    flag_ref[...] = worst

    for copy in a_copies + b_copies:
        copy.wait_recv()

    theirs = (1 - layer) * half
    mine = layer * half

    l_copies = []
    per = half // 2
    for c in range(2):
        @pl.loop(0, per, unroll=4)
        def _(k):
            r = theirs + c * per + k
            part[r] += product(1, a_in, b_in, r)

        l_copies.append(
            remote(
                part.at[pl.ds(theirs + c * per, per)], layer_in.at[pl.ds(c * per, per)],
                l_send.at[c], l_recv.at[c], at(0, 0, 1),
            )
        )

    @pl.loop(0, half, unroll=4)
    def _(k):
        r = mine + k
        part[r] += product(1, a_in, b_in, r)

    for c in range(2):
        l_copies[c].wait_recv()

        @pl.loop(0, per, unroll=2)
        def _(k):
            k = c * per + k
            total = (part[mine + k] + layer_in[k]).astype(out_ref.dtype)
            out_ref[k, 0] = total[:, : out_ref.shape[3]]
            out_ref[k, 1] = total[:, out_ref.shape[3] :]

    for copy in list(sends.values()) + a_copies + b_copies + l_copies:
        copy.wait_send()


def local(n_row, n_col, a_blocks, a_cols, a_count, b_blocks, b_cols, b_count, c_cols):
    a_panel, a_index, a_live = a_blocks[0, 0, 0], a_cols[0, 0, 0], a_count[0, 0, 0]
    b_panel, b_index, b_live = b_blocks[0, 0, 0], b_cols[0, 0, 0], b_count[0, 0, 0]
    out_cols = c_cols[0, 0]
    rows, ka, size, _ = a_panel.shape
    panel, kb, _, width = b_panel.shape
    kc = out_cols.shape[1]
    half = rows // 2
    lists = lists_of(a_index, a_live, b_index, b_live, out_cols)
    vmem = pltpu.VMEM
    dma = pltpu.SemaphoreType.DMA
    tile = (8, LANES)
    anywhere = pl.BlockSpec(memory_space=pl.ANY)
    in_vmem = pl.BlockSpec(memory_space=vmem)
    quick, worst = pl.pallas_call(
        functools.partial(kernel, n_row, n_col, panel, kb),
        out_shape=(
            jax.ShapeDtypeStruct((half, kc, size, width), jnp.bfloat16),
            jax.ShapeDtypeStruct(tile, jnp.int32),
        ),
        in_specs=[in_vmem, anywhere, anywhere],
        out_specs=(in_vmem, in_vmem),
        scratch_shapes=[
            vmem((rows * ka, size, size), jnp.bfloat16),
            vmem((panel * kb + 1, size, width), jnp.bfloat16),
            vmem((rows * ka, size, size), jnp.bfloat16),
            vmem((CAPACITY + 1, size, width), jnp.bfloat16),
            vmem((CAPACITY, size, width), jnp.bfloat16),
            vmem((rows, size, kc * width), jnp.float32),
            vmem((half, size, kc * width), jnp.float32),
            vmem((4,) + tile, jnp.int32),
            vmem((2,) + tile, jnp.int32),
            pltpu.SMEM((2,) + tile, jnp.int32),
            vmem((CAPACITY, LANES), jnp.int32),
            pltpu.SMEM((CAPACITY, LANES), jnp.int32),
            vmem(tile, jnp.int32),
            vmem(tile, jnp.int32),
            vmem(tile, jnp.int32),
            vmem((n_row - 1,) + tile, jnp.int32),
            vmem(tile, jnp.int32),
            vmem((n_col - 1,) + tile, jnp.int32),
            dma((4,)),
            dma((4,)), dma((4,)),
            dma((CHUNKS,)), dma((CHUNKS,)),
            dma((CHUNKS,)), dma((CHUNKS,)),
            dma((2,)), dma((2,)),
            dma((1,)), dma((1,)),
            dma((n_row - 1,)), dma((n_row - 1,)),
            dma((n_col - 1,)), dma((n_col - 1,)),
        ],
        compiler_params=pltpu.CompilerParams(
            collective_id=0, has_side_effects=True, vmem_limit_bytes=40 * 1024 * 1024
        ),
        cost_estimate=pl.CostEstimate(
            flops=4 * rows * size * ka * size * kc * width, bytes_accessed=6 << 20, transcendentals=0
        ),
    )(lists, a_panel.reshape(rows * ka, size, size), b_panel.reshape(panel * kb, size, width))
    result = lax.cond(
        worst[0, 0] > CAPACITY,
        lambda: general(a_panel, a_index, a_live, b_panel, b_index, b_live, out_cols),
        lambda: quick,
    )
    return result[None, None]


def solution(mesh):
    return jax.shard_map(
        functools.partial(local, mesh.shape["row"], mesh.shape["col"]),
        mesh=mesh,
        in_specs=(
            P("row", "col", "layer", None, None, None, None),
            P("row", "col", "layer", None, None),
            P("row", "col", "layer", None),
            P("row", "col", "layer", None, None, None, None),
            P("row", "col", "layer", None, None),
            P("row", "col", "layer", None),
            P("row", "col", None, None),
        ),
        out_specs=P("row", "col", "layer", None, None, None),
        check_vma=False,
    )
```

```python
import functools

import jax
import jax.numpy as jnp
from jax import lax
from jax.experimental import pallas as pl
from jax.experimental.pallas import tpu as pltpu
from jax.sharding import PartitionSpec as P

CAPACITY = 32
CHUNKS = 4
ABSENT = 1000
LANES = 128


def fill_lists(tile_ref, rows_ref, a_cols, a_count, b_cols, b_count, c_cols):
    ka, rows = a_cols.shape
    kc = c_cols.shape[0]
    kb, panel = b_cols.shape
    stride = panel // rows
    r = lax.broadcasted_iota(jnp.int32, (ka, rows), 1)
    t = lax.broadcasted_iota(jnp.int32, (ka, rows), 0)
    offset = a_cols[...] - stride * r + 1
    offset = jnp.where(offset < 0, offset + panel, offset)
    offset = jnp.where(offset >= panel, offset - panel, offset)
    u = lax.broadcasted_iota(jnp.int32, (kb, panel), 0)
    rows_ref[...] = jnp.full(rows_ref.shape, ABSENT, jnp.int32)
    rows_ref[0:ka, 0:rows] = jnp.where(t < a_count[...], offset, ABSENT)
    rows_ref[ka : ka + kc, 0:rows] = c_cols[...]
    rows_ref[ka + kc : ka + kc + kb, 0:panel] = jnp.where(u < b_count[...], b_cols[...], -1)
    columns = jnp.transpose(rows_ref[...])

    def along(height, source, column):
        place = lax.broadcasted_iota(jnp.int32, (height, LANES), 0)
        entries = jnp.broadcast_to(columns[:height, column : column + 1], (height, LANES))
        return jnp.sum(jnp.where(place == source(height), entries, 0), axis=0, keepdims=True)

    def own_row(height):
        return lax.broadcasted_iota(jnp.int32, (height, LANES), 1) // 4

    lane = lax.broadcasted_iota(jnp.int32, (1, LANES), 1)
    a_slots = [along(rows, own_row, k) for k in range(ka)]
    c_slots = [along(rows, own_row, ka + k) for k in range(kc)]
    tile_ref[0:1] = jnp.where(lane % 4 < 2, a_slots[0], a_slots[1])
    tile_ref[1:2] = jnp.where(lane % 2 == 0, c_slots[0], c_slots[1])
    for d in range(stride):

        def near(height):
            m = own_row(height) * stride + (d - 1)
            return jnp.where(m < 0, m + panel, m)

        for k in range(kb):
            row = 2 + d * kb + k
            tile_ref[row : row + 1] = along(panel, near, ka + kc + k)


def matched(a_row, c_row, b_rows, rows, panel, kb):
    shape = (8, LANES)
    stride = panel // rows
    lane = lax.broadcasted_iota(jnp.int32, shape, 1)
    r = lane // 4
    a_row = jnp.broadcast_to(a_row, shape)
    c_row = jnp.broadcast_to(c_row, shape)
    need = jnp.zeros(shape, jnp.int32)
    place = jnp.full(shape, panel * kb, jnp.int32)
    for d in range(stride):
        m = r * stride + (d - 1)
        m = jnp.where(m < 0, m + panel, m)
        for u in range(kb):
            k = d * kb + u
            hit = (a_row == d) & (c_row == jnp.broadcast_to(b_rows[k : k + 1], shape))
            hit = hit & (lane < rows * 4)
            need = jnp.where(hit, 1, need)
            place = jnp.where(hit, m * kb + u, place)
    return need, place


def earlier(need):
    lane = lax.broadcasted_iota(jnp.int32, need.shape, 1)
    total = need
    step = 1
    while step < LANES:
        total = total + jnp.where(lane >= step, pltpu.roll(total, step, 1), 0)
        step *= 2
    return total - need


def kernel(
    n_row, n_col, capacity,
    a_cols, a_count, b_cols, b_count, c_cols, a_hbm, b_hbm,
    out_ref, flag_ref,
    lists_ref, rows_ref,
    av, bv, a_in, b_in, packed, part, layer_in, tiles, table_v, table_s, send_v, send_s,
    flag_own, flag_layer, flag_row_src, flag_row, flag_col_src, flag_col,
    local_sem, list_send, list_recv, a_send, a_recv, b_send, b_recv, l_send, l_recv,
    f0_send, f0_recv, f1_send, f1_recv, f2_send, f2_recv,
):
    row = lax.axis_index("row")
    col = lax.axis_index("col")
    layer = lax.axis_index("layer")
    rows = out_ref.shape[0] * 2
    half = rows // 2
    kb, panel = b_cols.shape

    def at(d_row, d_col, d_layer=0):
        return {
            "row": lax.rem(row + d_row + n_row, n_row),
            "col": lax.rem(col + d_col + n_col, n_col),
            "layer": lax.rem(layer + d_layer, 2),
        }

    load_b = pltpu.make_async_copy(b_hbm, bv.at[pl.ds(0, panel * kb)], local_sem.at[0])
    load_b.start()
    load_a = pltpu.make_async_copy(a_hbm, av, local_sem.at[1])
    load_a.start()

    barrier = pltpu.get_barrier_semaphore()
    partners = [at(o, 0) for o in range(1, n_row)] + [at(0, o) for o in range(1, n_col)]
    partners += [at(0, 0, 1), at(1, -1), at(-1, 1)]
    for partner in partners:
        pl.semaphore_signal(barrier, inc=1, device_id=partner, device_id_type=pl.DeviceIdType.MESH)

    zero = jnp.zeros(bv.shape[1:], bv.dtype)
    bv[panel * kb] = zero
    b_in[capacity] = zero
    fill_lists(lists_ref, rows_ref, a_cols, a_count, b_cols, b_count, c_cols)
    own = lists_ref[...]
    need, place = matched(own[0:1], own[1:2], own[2:], rows, panel, kb)
    table_v[0] = place

    pl.semaphore_wait(barrier, len(partners))

    def remote(src, dst, send, recv, device):
        copy = pltpu.make_async_remote_copy(
            src_ref=src, dst_ref=dst, send_sem=send, recv_sem=recv,
            device_id=device, device_id_type=pl.DeviceIdType.MESH,
        )
        copy.start()
        return copy

    sends = {}
    for slot, device in ((2, at(1, 0)), (3, at(1, -1)), (1, at(-1, 0)), (0, at(0, -1))):
        sends[slot] = remote(lists_ref, tiles.at[slot], list_send.at[slot], list_recv.at[slot], device)
    a_copies = []
    per = av.shape[0] // CHUNKS
    for c in range(CHUNKS):
        piece = pl.ds(c * per, per)
        a_copies.append(
            remote(a_hbm.at[piece], a_in.at[piece], a_send.at[c], a_recv.at[c], at(0, -1))
        )

    sends[2].wait_recv()
    sends[3].wait_recv()
    need, place = matched(tiles[3, 0:1], tiles[2, 1:2], own[2:], rows, panel, kb)
    before = earlier(need)
    wanted = lax.broadcasted_iota(jnp.int32, (capacity, LANES), 0)
    spread = (capacity, LANES)
    here = (jnp.broadcast_to(before[0:1], spread) == wanted) & (
        jnp.broadcast_to(need[0:1], spread) > 0
    )
    chosen = jnp.sum(jnp.where(here, jnp.broadcast_to(place[0:1], spread), 0), axis=1, keepdims=True)
    send_v[...] = jnp.broadcast_to(chosen, spread)
    to_smem = pltpu.make_async_copy(send_v, send_s, local_sem.at[2])
    to_smem.start()
    lane = lax.broadcasted_iota(jnp.int32, (8, LANES), 1)
    last = jnp.where(lane == LANES - 1, before + need, 0)
    flag_own[...] = jnp.broadcast_to(jnp.max(last, axis=1, keepdims=True), (8, LANES))
    load_b.wait()
    to_smem.wait()
    b_copies = []
    per = capacity // CHUNKS
    for c in range(CHUNKS):
        for k in range(c * per, (c + 1) * per):
            packed[k] = bv[send_s[k, 0]]
        piece = pl.ds(c * per, per)
        b_copies.append(
            remote(packed.at[piece], b_in.at[piece], b_send.at[c], b_recv.at[c], at(-1, 0))
        )
    f0 = remote(flag_own, flag_layer, f0_send.at[0], f0_recv.at[0], at(0, 0, 1))

    sends[0].wait_recv()
    sends[1].wait_recv()
    need, place = matched(tiles[0, 0:1], own[1:2], tiles[1][2:], rows, panel, kb)
    before = earlier(need)
    table_v[1] = jnp.where((need > 0) & (before < capacity), before, capacity)
    to_smem = pltpu.make_async_copy(table_v, table_s, local_sem.at[3])
    to_smem.start()

    f0.wait()
    flag_row_src[...] = jnp.maximum(flag_own[...], flag_layer[...])
    f1 = [
        remote(flag_row_src, flag_row.at[o - 1], f1_send.at[o - 1], f1_recv.at[o - 1], at(o, 0))
        for o in range(1, n_row)
    ]
    to_smem.wait()
    load_a.wait()

    def product(step, a, b, r):
        block = [b[table_s[step, 0, 4 * r + k]] for k in range(4)]
        left = jnp.concatenate([a[2 * r], a[2 * r + 1]], axis=1)
        right = jnp.concatenate(
            [jnp.concatenate(block[:2], axis=1), jnp.concatenate(block[2:], axis=1)], axis=0
        )
        return jnp.dot(left, right, preferred_element_type=jnp.float32)

    @pl.loop(0, rows, unroll=4)
    def _(r):
        part[r] = product(0, av, bv, r)

    worst = flag_row_src[...]
    for o in range(1, n_row):
        f1[o - 1].wait()
        worst = jnp.maximum(worst, flag_row[o - 1])
    flag_col_src[...] = worst
    f2 = [
        remote(flag_col_src, flag_col.at[o - 1], f2_send.at[o - 1], f2_recv.at[o - 1], at(0, o))
        for o in range(1, n_col)
    ]
    for o in range(1, n_col):
        f2[o - 1].wait()
        worst = jnp.maximum(worst, flag_col[o - 1])
    flag_ref[...] = jnp.where(worst[0:1, 0:1] > capacity, 1, 0)

    for copy in a_copies + b_copies:
        copy.wait_recv()

    theirs = (1 - layer) * half
    mine = layer * half

    l_copies = []
    per = half // 2
    for c in range(2):
        @pl.loop(0, per, unroll=4)
        def _(k):
            r = theirs + c * per + k
            part[r] += product(1, a_in, b_in, r)

        l_copies.append(
            remote(
                part.at[pl.ds(theirs + c * per, per)], layer_in.at[pl.ds(c * per, per)],
                l_send.at[c], l_recv.at[c], at(0, 0, 1),
            )
        )

    @pl.loop(0, half, unroll=4)
    def _(k):
        r = mine + k
        part[r] += product(1, a_in, b_in, r)

    for c in range(2):
        l_copies[c].wait_recv()

        @pl.loop(0, per, unroll=2)
        def _(k):
            k = c * per + k
            total = (part[mine + k] + layer_in[k]).astype(out_ref.dtype)
            out_ref[k, 0] = total[:, : out_ref.shape[3]]
            out_ref[k, 1] = total[:, out_ref.shape[3] :]

    for copy in list(sends.values()) + a_copies + b_copies + l_copies:
        copy.wait_send()


def call(n_row, n_col, capacity, collective_id, a_cols, a_count, b_cols, b_count, c_cols, a, b):
    ka, rows = a_cols.shape
    kb, panel = b_cols.shape
    kc = c_cols.shape[0]
    size, width = a.shape[1], b.shape[2]
    half = rows // 2
    vmem = pltpu.VMEM
    dma = pltpu.SemaphoreType.DMA
    tile = (8, LANES)
    anywhere = pl.BlockSpec(memory_space=pl.ANY)
    in_vmem = pl.BlockSpec(memory_space=vmem)
    return pl.pallas_call(
        functools.partial(kernel, n_row, n_col, capacity),
        out_shape=(
            jax.ShapeDtypeStruct((half, kc, size, width), jnp.bfloat16),
            jax.ShapeDtypeStruct((1, 1), jnp.int32),
        ),
        in_specs=[in_vmem] * 5 + [anywhere] * 2,
        out_specs=(in_vmem, in_vmem),
        scratch_shapes=[
            vmem(tile, jnp.int32),
            vmem(tile, jnp.int32),
            vmem((rows * ka, size, size), jnp.bfloat16),
            vmem((panel * kb + 1, size, width), jnp.bfloat16),
            vmem((rows * ka, size, size), jnp.bfloat16),
            vmem((capacity + 1, size, width), jnp.bfloat16),
            vmem((capacity, size, width), jnp.bfloat16),
            vmem((rows, size, kc * width), jnp.float32),
            vmem((half, size, kc * width), jnp.float32),
            vmem((4,) + tile, jnp.int32),
            vmem((2,) + tile, jnp.int32),
            pltpu.SMEM((2,) + tile, jnp.int32),
            vmem((capacity, LANES), jnp.int32),
            pltpu.SMEM((capacity, LANES), jnp.int32),
            vmem(tile, jnp.int32),
            vmem(tile, jnp.int32),
            vmem(tile, jnp.int32),
            vmem((n_row - 1,) + tile, jnp.int32),
            vmem(tile, jnp.int32),
            vmem((n_col - 1,) + tile, jnp.int32),
            dma((4,)),
            dma((4,)), dma((4,)),
            dma((CHUNKS,)), dma((CHUNKS,)),
            dma((CHUNKS,)), dma((CHUNKS,)),
            dma((2,)), dma((2,)),
            dma((1,)), dma((1,)),
            dma((n_row - 1,)), dma((n_row - 1,)),
            dma((n_col - 1,)), dma((n_col - 1,)),
        ],
        compiler_params=pltpu.CompilerParams(
            collective_id=collective_id, has_side_effects=True, vmem_limit_bytes=40 * 1024 * 1024
        ),
        cost_estimate=pl.CostEstimate(
            flops=4 * rows * size * ka * size * kc * width, bytes_accessed=6 << 20, transcendentals=0
        ),
    )(a_cols, a_count, b_cols, b_count, c_cols, a, b)


def local(n_row, n_col, a_blocks, a_cols, a_count, b_blocks, b_cols, b_count, c_cols):
    a_panel, b_panel = a_blocks[0, 0, 0], b_blocks[0, 0, 0]
    args = (
        a_cols[0, 0, 0].T, a_count[0, 0], b_cols[0, 0, 0].T, b_count[0, 0], c_cols[0, 0].T,
        a_panel.reshape((-1,) + a_panel.shape[2:]), b_panel.reshape((-1,) + b_panel.shape[2:]),
    )
    every = a_panel.shape[0] * a_panel.shape[1] * c_cols.shape[3]
    quick, over = call(n_row, n_col, CAPACITY, 0, *args)
    result = lax.cond(
        over[0, 0] > 0,
        lambda args, quick: call(n_row, n_col, every, 1, *args)[0],
        lambda args, quick: quick,
        args, quick,
    )
    return result[None, None]


def solution(mesh):
    return jax.shard_map(
        functools.partial(local, mesh.shape["row"], mesh.shape["col"]),
        mesh=mesh,
        in_specs=(
            P("row", "col", "layer", None, None, None, None),
            P("row", "col", "layer", None, None),
            P("row", "col", "layer", None),
            P("row", "col", "layer", None, None, None, None),
            P("row", "col", "layer", None, None),
            P("row", "col", "layer", None),
            P("row", "col", None, None),
        ),
        out_specs=P("row", "col", "layer", None, None, None),
        check_vma=False,
    )
```

```python
import functools

import jax
import jax.numpy as jnp
from jax import lax
from jax.experimental import pallas as pl
from jax.experimental.pallas import tpu as pltpu
from jax.sharding import PartitionSpec as P

CAPACITY = 32
CHUNKS = 4
ABSENT = 1000
LANES = 128


def block_row(lane, rows):
    q = lane // 4
    return (q % 2) * (rows // 2) + q // 2


def fill_lists(tile_ref, rows_ref, a_cols, a_count, b_cols, b_count, c_cols):
    ka, rows = a_cols.shape
    kc = c_cols.shape[0]
    kb, panel = b_cols.shape
    stride = panel // rows
    r = lax.broadcasted_iota(jnp.int32, (ka, rows), 1)
    t = lax.broadcasted_iota(jnp.int32, (ka, rows), 0)
    offset = a_cols[...] - stride * r + 1
    offset = jnp.where(offset < 0, offset + panel, offset)
    offset = jnp.where(offset >= panel, offset - panel, offset)
    u = lax.broadcasted_iota(jnp.int32, (kb, panel), 0)
    rows_ref[...] = jnp.full(rows_ref.shape, ABSENT, jnp.int32)
    rows_ref[0:ka, 0:rows] = jnp.where(t < a_count[...], offset, ABSENT)
    rows_ref[ka : ka + kc, 0:rows] = c_cols[...]
    rows_ref[ka + kc : ka + kc + kb, 0:panel] = jnp.where(u < b_count[...], b_cols[...], -1)
    columns = jnp.transpose(rows_ref[...])

    def along(height, source, column):
        place = lax.broadcasted_iota(jnp.int32, (height, LANES), 0)
        entries = jnp.broadcast_to(columns[:height, column : column + 1], (height, LANES))
        return jnp.sum(jnp.where(place == source(height), entries, 0), axis=0, keepdims=True)

    def own_row(height):
        return block_row(lax.broadcasted_iota(jnp.int32, (height, LANES), 1), rows)

    lane = lax.broadcasted_iota(jnp.int32, (1, LANES), 1)
    a_slots = [along(rows, own_row, k) for k in range(ka)]
    c_slots = [along(rows, own_row, ka + k) for k in range(kc)]
    tile_ref[0:1] = jnp.where(lane % 4 < 2, a_slots[0], a_slots[1])
    tile_ref[1:2] = jnp.where(lane % 2 == 0, c_slots[0], c_slots[1])
    for d in range(stride):

        def near(height):
            m = own_row(height) * stride + (d - 1)
            return jnp.where(m < 0, m + panel, m)

        for k in range(kb):
            row = 2 + d * kb + k
            tile_ref[row : row + 1] = along(panel, near, ka + kc + k)


def matched(a_row, c_row, b_rows, rows, panel, kb):
    shape = (8, LANES)
    stride = panel // rows
    lane = lax.broadcasted_iota(jnp.int32, shape, 1)
    r = block_row(lane, rows)
    a_row = jnp.broadcast_to(a_row, shape)
    c_row = jnp.broadcast_to(c_row, shape)
    need = jnp.zeros(shape, jnp.int32)
    place = jnp.full(shape, panel * kb, jnp.int32)
    for d in range(stride):
        m = r * stride + (d - 1)
        m = jnp.where(m < 0, m + panel, m)
        for u in range(kb):
            k = d * kb + u
            hit = (a_row == d) & (c_row == jnp.broadcast_to(b_rows[k : k + 1], shape))
            hit = hit & (lane < rows * 4)
            need = jnp.where(hit, 1, need)
            place = jnp.where(hit, m * kb + u, place)
    return need, place


def earlier(need):
    lane = lax.broadcasted_iota(jnp.int32, need.shape, 1)
    total = need
    step = 1
    while step < LANES:
        total = total + jnp.where(lane >= step, pltpu.roll(total, step, 1), 0)
        step *= 2
    return total - need


def kernel(
    n_row, n_col, capacity,
    a_cols_hbm, a_count_hbm, b_cols_hbm, b_count_hbm, c_cols_hbm, a_hbm, b_hbm,
    out_ref, flag_ref,
    a_cols, a_count, b_cols, b_count, c_cols,
    lists_ref, rows_ref,
    av, bv, a_in, b_first, b_last, packed, part, layer_in, tiles, table_v, table_s, send_v, send_s,
    flag_own, flag_layer, flag_row_src, flag_row, flag_col_src, flag_col,
    local_sem, list_send, list_recv, a_send, a_recv, b_send, b_recv, l_send, l_recv,
    f0_send, f0_recv, f1_send, f1_recv, f2_send, f2_recv,
):
    row = lax.axis_index("row")
    col = lax.axis_index("col")
    layer = lax.axis_index("layer")
    rows = out_ref.shape[0] * 2
    half = rows // 2
    kb, panel = b_cols.shape

    def at(d_row, d_col, d_layer=0):
        return {
            "row": lax.rem(row + d_row + n_row, n_row),
            "col": lax.rem(col + d_col + n_col, n_col),
            "layer": lax.rem(layer + d_layer, 2),
        }

    barrier = pltpu.get_barrier_semaphore()
    partners = [at(o, 0) for o in range(1, n_row)] + [at(0, o) for o in range(1, n_col)]
    partners += [at(0, 0, 1), at(1, -1), at(-1, 1)]
    for partner in partners:
        pl.semaphore_signal(barrier, inc=1, device_id=partner, device_id_type=pl.DeviceIdType.MESH)

    loads = [
        pltpu.make_async_copy(src, dst, local_sem.at[4 + k])
        for k, (src, dst) in enumerate((
            (a_cols_hbm, a_cols), (a_count_hbm, a_count), (b_cols_hbm, b_cols),
            (b_count_hbm, b_count), (c_cols_hbm, c_cols),
        ))
    ]
    for load in loads:
        load.start()
    load_b = pltpu.make_async_copy(b_hbm, bv.at[pl.ds(0, panel * kb)], local_sem.at[0])
    load_b.start()
    load_a = pltpu.make_async_copy(a_hbm, av, local_sem.at[1])
    load_a.start()
    per = capacity // CHUNKS
    first = capacity - per
    zero = jnp.zeros(bv.shape[1:], bv.dtype)
    bv[panel * kb] = zero
    b_first[first] = zero
    b_last[per] = zero
    for load in loads:
        load.wait()
    fill_lists(lists_ref, rows_ref, a_cols, a_count, b_cols, b_count, c_cols)
    own = lists_ref[...]
    need, place = matched(own[0:1], own[1:2], own[2:], rows, panel, kb)
    table_v[0:1] = place[0:1]

    pl.semaphore_wait(barrier, len(partners))

    def remote(src, dst, send, recv, device):
        copy = pltpu.make_async_remote_copy(
            src_ref=src, dst_ref=dst, send_sem=send, recv_sem=recv,
            device_id=device, device_id_type=pl.DeviceIdType.MESH,
        )
        copy.start()
        return copy

    sends = {}
    for slot, device in ((2, at(1, 0)), (3, at(1, -1)), (1, at(-1, 0)), (0, at(0, -1))):
        sends[slot] = remote(lists_ref, tiles.at[slot], list_send.at[slot], list_recv.at[slot], device)
    a_copies = []
    a_per = av.shape[0] // CHUNKS
    for c in range(CHUNKS):
        piece = pl.ds(c * a_per, a_per)
        a_copies.append(
            remote(a_hbm.at[piece], a_in.at[piece], a_send.at[c], a_recv.at[c], at(0, -1))
        )

    sends[2].wait_recv()
    sends[3].wait_recv()
    need, place = matched(tiles[3, 0:1], tiles[2, 1:2], own[2:], rows, panel, kb)
    spread = (rows * 4, LANES)
    lane = lax.broadcasted_iota(jnp.int32, spread, 1)
    entry = lax.broadcasted_iota(jnp.int32, spread, 0)
    needed = jnp.broadcast_to(need[0:1], spread)
    before = jnp.sum(jnp.where(lane < entry, needed, 0), axis=1, keepdims=True)
    taken = jnp.where(lane == entry, needed * (1 + jnp.broadcast_to(place[0:1], spread)), 0)
    taken = jnp.broadcast_to(jnp.sum(taken, axis=1, keepdims=True), spread)
    here = (jnp.broadcast_to(before, spread) == lane) & (taken > 0)
    send_v[...] = jnp.sum(jnp.where(here, taken - 1, 0), axis=0, keepdims=True)
    to_smem = pltpu.make_async_copy(send_v, send_s, local_sem.at[2])
    to_smem.start()
    flag_own[...] = jnp.broadcast_to(jnp.sum(need, axis=1, keepdims=True), flag_own.shape)
    load_b.wait()
    to_smem.wait()
    b_copies = []
    for c in range(CHUNKS):
        for k in range(c * per, (c + 1) * per):
            packed[k] = bv[send_s[0, k]]
        piece = pl.ds(c * per, per)
        landing = b_first.at[piece] if c < CHUNKS - 1 else b_last.at[pl.ds(0, per)]
        b_copies.append(
            remote(packed.at[piece], landing, b_send.at[c], b_recv.at[c], at(-1, 0))
        )
    f0 = remote(flag_own, flag_layer, f0_send.at[0], f0_recv.at[0], at(0, 0, 1))

    sends[0].wait_recv()
    sends[1].wait_recv()
    need, place = matched(tiles[0, 0:1], own[1:2], tiles[1][2:], rows, panel, kb)
    before = earlier(need)
    table_v[1:2] = jnp.where((need > 0) & (before < capacity), before, capacity)[0:1]
    to_smem = pltpu.make_async_copy(table_v, table_s, local_sem.at[3])
    to_smem.start()

    f0.wait()
    flag_row_src[...] = jnp.maximum(flag_own[...], flag_layer[...])
    f1 = [
        remote(flag_row_src, flag_row.at[o - 1], f1_send.at[o - 1], f1_recv.at[o - 1], at(o, 0))
        for o in range(1, n_row)
    ]
    to_smem.wait()
    load_a.wait()

    def blocks_of(step, r):
        q = 2 * lax.rem(r, half) + r // half
        return [table_s[step, 4 * q + k] for k in range(4)]

    def from_first(place):
        return b_first[jnp.where(place < first, place, first)]

    def from_all(place):
        last = jnp.where(place < first, per, place - first)
        return jnp.where(place < first, from_first(place), b_last[last])

    def product(a, block, r):
        left = jnp.concatenate([a[2 * r], a[2 * r + 1]], axis=1)
        right = jnp.concatenate(
            [jnp.concatenate(block[:2], axis=1), jnp.concatenate(block[2:], axis=1)], axis=0
        )
        return jnp.dot(left, right, preferred_element_type=jnp.float32)

    @pl.loop(0, rows, unroll=4)
    def _(r):
        part[r] = product(av, [bv[place] for place in blocks_of(0, r)], r)

    worst = flag_row_src[...]
    for o in range(1, n_row):
        f1[o - 1].wait()
        worst = jnp.maximum(worst, flag_row[o - 1])
    flag_col_src[...] = worst
    f2 = [
        remote(flag_col_src, flag_col.at[o - 1], f2_send.at[o - 1], f2_recv.at[o - 1], at(0, o))
        for o in range(1, n_col)
    ]
    for o in range(1, n_col):
        f2[o - 1].wait()
        worst = jnp.maximum(worst, flag_col[o - 1])
    flag_ref[...] = jnp.where(worst[0:1, 0:1] > capacity, 1, 0)

    theirs = (1 - layer) * half
    mine = layer * half
    early = first // 8
    middle = (early + half + 1) // 2
    l_copies = []

    def add_step(base, low, high, read):
        @pl.loop(low, high, unroll=high - low)
        def _(k):
            r = base + k
            part[r] += product(a_in, [read(place) for place in blocks_of(1, r)], r)

    def hand_over(low, high):
        c = len(l_copies)
        l_copies.append(
            remote(
                part.at[pl.ds(theirs + low, high - low)], layer_in.at[pl.ds(low, high - low)],
                l_send.at[c], l_recv.at[c], at(0, 0, 1),
            )
        )

    for copy in a_copies + b_copies[:-1]:
        copy.wait_recv()
    add_step(theirs, 0, early, from_first)
    hand_over(0, early)
    add_step(mine, 0, early, from_first)

    b_copies[-1].wait_recv()
    add_step(theirs, early, middle, from_all)
    hand_over(early, middle)
    add_step(theirs, middle, half, from_all)
    hand_over(middle, half)
    add_step(mine, early, half, from_all)

    for copy, (low, high) in zip(l_copies, ((0, early), (early, middle), (middle, half))):
        copy.wait_recv()

        @pl.loop(low, high, unroll=high - low)
        def _(k):
            total = (part[mine + k] + layer_in[k]).astype(out_ref.dtype)
            out_ref[k, 0] = total[:, : out_ref.shape[3]]
            out_ref[k, 1] = total[:, out_ref.shape[3] :]

    for copy in list(sends.values()) + a_copies + b_copies + l_copies:
        copy.wait_send()


def call(n_row, n_col, capacity, collective_id, a_cols, a_count, b_cols, b_count, c_cols, a, b):
    ka, rows = a_cols.shape
    kb, panel = b_cols.shape
    kc = c_cols.shape[0]
    size, width = a.shape[1], b.shape[2]
    half = rows // 2
    per = capacity // CHUNKS
    vmem = pltpu.VMEM
    dma = pltpu.SemaphoreType.DMA
    tile = (8, LANES)
    anywhere = pl.BlockSpec(memory_space=pl.ANY)
    in_vmem = pl.BlockSpec(memory_space=vmem)
    return pl.pallas_call(
        functools.partial(kernel, n_row, n_col, capacity),
        out_shape=(
            jax.ShapeDtypeStruct((half, kc, size, width), jnp.bfloat16),
            jax.ShapeDtypeStruct((1, 1), jnp.int32),
        ),
        in_specs=[anywhere] * 7,
        out_specs=(in_vmem, in_vmem),
        scratch_shapes=[
            vmem(a_cols.shape, jnp.int32),
            vmem(a_count.shape, jnp.int32),
            vmem(b_cols.shape, jnp.int32),
            vmem(b_count.shape, jnp.int32),
            vmem(c_cols.shape, jnp.int32),
            vmem(tile, jnp.int32),
            vmem(tile, jnp.int32),
            vmem((rows * ka, size, size), jnp.bfloat16),
            vmem((panel * kb + 1, size, width), jnp.bfloat16),
            vmem((rows * ka, size, size), jnp.bfloat16),
            vmem((capacity - per + 1, size, width), jnp.bfloat16),
            vmem((per + 1, size, width), jnp.bfloat16),
            vmem((capacity, size, width), jnp.bfloat16),
            vmem((rows, size, kc * width), jnp.float32),
            vmem((half, size, kc * width), jnp.float32),
            vmem((4,) + tile, jnp.int32),
            vmem((2, LANES), jnp.int32),
            pltpu.SMEM((2, LANES), jnp.int32),
            vmem((1, LANES), jnp.int32),
            pltpu.SMEM((1, LANES), jnp.int32),
            vmem(tile, jnp.int32),
            vmem(tile, jnp.int32),
            vmem(tile, jnp.int32),
            vmem((n_row - 1,) + tile, jnp.int32),
            vmem(tile, jnp.int32),
            vmem((n_col - 1,) + tile, jnp.int32),
            dma((9,)),
            dma((4,)), dma((4,)),
            dma((CHUNKS,)), dma((CHUNKS,)),
            dma((CHUNKS,)), dma((CHUNKS,)),
            dma((3,)), dma((3,)),
            dma((1,)), dma((1,)),
            dma((n_row - 1,)), dma((n_row - 1,)),
            dma((n_col - 1,)), dma((n_col - 1,)),
        ],
        compiler_params=pltpu.CompilerParams(
            collective_id=collective_id, has_side_effects=True, vmem_limit_bytes=40 * 1024 * 1024
        ),
        cost_estimate=pl.CostEstimate(
            flops=4 * rows * size * ka * size * kc * width, bytes_accessed=6 << 20, transcendentals=0
        ),
    )(a_cols, a_count, b_cols, b_count, c_cols, a, b)


def local(n_row, n_col, a_blocks, a_cols, a_count, b_blocks, b_cols, b_count, c_cols):
    a_panel, b_panel = a_blocks[0, 0, 0], b_blocks[0, 0, 0]
    args = (
        a_cols[0, 0, 0].T, a_count[0, 0], b_cols[0, 0, 0].T, b_count[0, 0], c_cols[0, 0].T,
        a_panel.reshape((-1,) + a_panel.shape[2:]), b_panel.reshape((-1,) + b_panel.shape[2:]),
    )
    every = a_panel.shape[0] * a_panel.shape[1] * c_cols.shape[3]
    quick, over = call(n_row, n_col, CAPACITY, 0, *args)
    result = lax.cond(
        over[0, 0] > 0,
        lambda args, quick: call(n_row, n_col, every, 1, *args)[0],
        lambda args, quick: quick,
        args, quick,
    )
    return result[None, None]


def solution(mesh):
    return jax.shard_map(
        functools.partial(local, mesh.shape["row"], mesh.shape["col"]),
        mesh=mesh,
        in_specs=(
            P("row", "col", "layer", None, None, None, None),
            P("row", "col", "layer", None, None),
            P("row", "col", "layer", None),
            P("row", "col", "layer", None, None, None, None),
            P("row", "col", "layer", None, None),
            P("row", "col", "layer", None),
            P("row", "col", None, None),
        ),
        out_specs=P("row", "col", "layer", None, None, None),
        check_vma=False,
    )
```

```python
import functools

import jax
import jax.numpy as jnp
from jax import lax
from jax.experimental import pallas as pl
from jax.experimental.pallas import tpu as pltpu
from jax.sharding import PartitionSpec as P

SLOTS = 28
WINDOW = 4
CHUNKS = 4
ABSENT = 1000
LANES = 128


def block_row(lane, rows):
    q = lane // 4
    return (q % 2) * (rows // 2) + q // 2


def fill_lists(tile_ref, rows_ref, a_cols, a_count, b_cols, b_count, c_cols):
    ka, rows = a_cols.shape
    kc = c_cols.shape[0]
    kb, panel = b_cols.shape
    stride = panel // rows
    r = lax.broadcasted_iota(jnp.int32, (ka, rows), 1)
    t = lax.broadcasted_iota(jnp.int32, (ka, rows), 0)
    offset = a_cols[...] - stride * r + 1
    offset = jnp.where(offset < 0, offset + panel, offset)
    offset = jnp.where(offset >= panel, offset - panel, offset)
    u = lax.broadcasted_iota(jnp.int32, (kb, panel), 0)
    rows_ref[...] = jnp.full(rows_ref.shape, ABSENT, jnp.int32)
    rows_ref[0:ka, 0:rows] = jnp.where(t < a_count[...], offset, ABSENT)
    rows_ref[ka : ka + kc, 0:rows] = c_cols[...]
    rows_ref[ka + kc : ka + kc + kb, 0:panel] = jnp.where(u < b_count[...], b_cols[...], -1)
    columns = jnp.transpose(rows_ref[...])

    def along(height, source, column):
        place = lax.broadcasted_iota(jnp.int32, (height, LANES), 0)
        entries = jnp.broadcast_to(columns[:height, column : column + 1], (height, LANES))
        return jnp.sum(jnp.where(place == source(height), entries, 0), axis=0, keepdims=True)

    def own_row(height):
        return block_row(lax.broadcasted_iota(jnp.int32, (height, LANES), 1), rows)

    lane = lax.broadcasted_iota(jnp.int32, (1, LANES), 1)
    a_slots = [along(rows, own_row, k) for k in range(ka)]
    c_slots = [along(rows, own_row, ka + k) for k in range(kc)]
    tile_ref[0:1] = jnp.where(lane % 4 < 2, a_slots[0], a_slots[1])
    tile_ref[1:2] = jnp.where(lane % 2 == 0, c_slots[0], c_slots[1])
    for d in range(stride):

        def near(height):
            m = own_row(height) * stride + (d - 1)
            return jnp.where(m < 0, m + panel, m)

        for k in range(kb):
            row = 2 + d * kb + k
            tile_ref[row : row + 1] = along(panel, near, ka + kc + k)


def matched(a_row, c_row, b_rows, rows, panel, kb):
    shape = (8, LANES)
    stride = panel // rows
    lane = lax.broadcasted_iota(jnp.int32, shape, 1)
    r = block_row(lane, rows)
    a_row = jnp.broadcast_to(a_row, shape)
    c_row = jnp.broadcast_to(c_row, shape)
    need = jnp.zeros(shape, jnp.int32)
    place = jnp.full(shape, panel * kb, jnp.int32)
    for d in range(stride):
        m = r * stride + (d - 1)
        m = jnp.where(m < 0, m + panel, m)
        for u in range(kb):
            k = d * kb + u
            hit = (a_row == d) & (c_row == jnp.broadcast_to(b_rows[k : k + 1], shape))
            hit = hit & (lane < rows * 4)
            need = jnp.where(hit, 1, need)
            place = jnp.where(hit, m * kb + u, place)
    return need, place


def earlier(need):
    lane = lax.broadcasted_iota(jnp.int32, need.shape, 1)
    total = need
    step = 1
    while step < LANES:
        total = total + jnp.where(lane >= step, pltpu.roll(total, step, 1), 0)
        step *= 2
    return total - need


def kernel(
    n_row, n_col, slots, window, first,
    a_cols_hbm, a_count_hbm, b_cols_hbm, b_count_hbm, c_cols_hbm, a_hbm, b_hbm,
    out_ref, flag_ref,
    a_cols, a_count, b_cols, b_count, c_cols,
    lists_ref, rows_ref,
    av, bv, a_in, b_first, b_last, packed, extra, extra_in, part, layer_in, tiles, table_v, table_s, send_v, send_s,
    flag_own, flag_layer, flag_row_src, flag_row, flag_col_src, flag_col,
    local_sem, list_send, list_recv, a_send, a_recv, b_send, b_recv, e_send, e_recv, l_send, l_recv,
    f0_send, f0_recv, f1_send, f1_recv, f2_send, f2_recv,
):
    row = lax.axis_index("row")
    col = lax.axis_index("col")
    layer = lax.axis_index("layer")
    rows = out_ref.shape[0] * 2
    half = rows // 2
    kb, panel = b_cols.shape
    capacity = slots + window

    def at(d_row, d_col, d_layer=0):
        return {
            "row": lax.rem(row + d_row + n_row, n_row),
            "col": lax.rem(col + d_col + n_col, n_col),
            "layer": lax.rem(layer + d_layer, 2),
        }

    loads = [
        pltpu.make_async_copy(src, dst, local_sem.at[4 + k])
        for k, (src, dst) in enumerate((
            (a_cols_hbm, a_cols), (a_count_hbm, a_count), (b_cols_hbm, b_cols),
            (b_count_hbm, b_count), (c_cols_hbm, c_cols),
        ))
    ]
    for load in loads:
        load.start()

    barrier = pltpu.get_barrier_semaphore()
    partners = [at(o, 0) for o in range(1, n_row)] + [at(0, o) for o in range(1, n_col)]
    partners += [at(0, 0, 1), at(1, -1), at(-1, 1)]
    for partner in partners:
        pl.semaphore_signal(barrier, inc=1, device_id=partner, device_id_type=pl.DeviceIdType.MESH)

    zero = jnp.zeros(bv.shape[1:], bv.dtype)
    bv[panel * kb] = zero
    b_first[first] = zero
    b_last[capacity - first] = zero
    for load in loads:
        load.wait()
    load_b = pltpu.make_async_copy(b_hbm, bv.at[pl.ds(0, panel * kb)], local_sem.at[0])
    load_b.start()
    load_a = pltpu.make_async_copy(a_hbm, av, local_sem.at[1])
    load_a.start()
    fill_lists(lists_ref, rows_ref, a_cols, a_count, b_cols, b_count, c_cols)
    own = lists_ref[...]
    need, place = matched(own[0:1], own[1:2], own[2:], rows, panel, kb)
    table_v[0:1] = place[0:1]

    pl.semaphore_wait(barrier, len(partners))

    def remote(src, dst, send, recv, device):
        copy = pltpu.make_async_remote_copy(
            src_ref=src, dst_ref=dst, send_sem=send, recv_sem=recv,
            device_id=device, device_id_type=pl.DeviceIdType.MESH,
        )
        copy.start()
        return copy

    sends = {}
    for slot, device in ((2, at(1, 0)), (3, at(1, -1)), (1, at(-1, 0)), (0, at(0, -1))):
        sends[slot] = remote(lists_ref, tiles.at[slot], list_send.at[slot], list_recv.at[slot], device)
    a_copies = []
    a_per = av.shape[0] // CHUNKS
    for c in (0, CHUNKS // 2, 1, CHUNKS // 2 + 1):
        piece = pl.ds(c * a_per, a_per)
        a_copies.append(
            remote(a_hbm.at[piece], a_in.at[piece], a_send.at[c], a_recv.at[c], at(0, -1))
        )

    sends[2].wait_recv()
    sends[3].wait_recv()
    need, place = matched(tiles[3, 0:1], tiles[2, 1:2], own[2:], rows, panel, kb)
    spread = (rows * 4, LANES)
    lane = lax.broadcasted_iota(jnp.int32, spread, 1)
    entry = lax.broadcasted_iota(jnp.int32, spread, 0)
    needed = jnp.broadcast_to(need[0:1], spread)
    before = jnp.sum(jnp.where(lane < entry, needed, 0), axis=1, keepdims=True)
    taken = jnp.where(lane == entry, needed * (1 + jnp.broadcast_to(place[0:1], spread)), 0)
    taken = jnp.broadcast_to(jnp.sum(taken, axis=1, keepdims=True), spread)
    here = (jnp.broadcast_to(before, spread) == lane) & (taken > 0)
    count = jnp.sum(need, axis=1, keepdims=True)
    chosen = jnp.sum(jnp.where(here, taken - 1, 0), axis=0, keepdims=True)
    send_v[...] = jnp.where(lane[0:1] == LANES - 1, count[0:1], chosen)
    to_smem = pltpu.make_async_copy(send_v, send_s, local_sem.at[2])
    to_smem.start()
    flag_own[...] = jnp.broadcast_to(count, flag_own.shape)
    load_b.wait()
    to_smem.wait()
    if window:
        for k in range(window):
            extra[k] = bv[send_s[0, slots + k]]
        handed = remote(extra, extra_in, e_send.at[0], e_recv.at[0], at(0, 0, 1))
    b_copies = []

    def send_b(low, high):
        c = len(b_copies)
        into, start = (b_first, low) if low < first else (b_last, low - first)
        landing = into.at[pl.ds(start, high - low)]
        b_copies.append(
            remote(packed.at[pl.ds(low, high - low)], landing, b_send.at[c], b_recv.at[c], at(-1, 0))
        )

    body = slots - window
    for low, high in ((0, first // 2), (first // 2, first)):
        for k in range(low, high):
            packed[k] = bv[send_s[0, k]]
        send_b(low, high)
    if window:
        handed.wait_recv()
        for k in range(body, slots):
            packed[k] = jnp.where(k < send_s[0, LANES - 1], bv[send_s[0, k]], extra_in[slots - 1 - k])
        send_b(body, slots)
    for k in range(first, body):
        packed[k] = bv[send_s[0, k]]
    send_b(first, body)
    f0 = remote(flag_own, flag_layer, f0_send.at[0], f0_recv.at[0], at(0, 0, 1))

    sends[0].wait_recv()
    sends[1].wait_recv()
    need, place = matched(tiles[0, 0:1], own[1:2], tiles[1][2:], rows, panel, kb)
    before = earlier(need)
    before = jnp.where((need > 0) & (before < capacity), before, capacity)
    back = (before >= slots) & (before < capacity)
    table_v[1:2] = jnp.where(back, slots + capacity - 1 - before, before)[0:1]
    to_smem = pltpu.make_async_copy(table_v, table_s, local_sem.at[3])
    to_smem.start()

    f0.wait()
    crowded = jnp.maximum(flag_own[...], flag_layer[...]) > capacity
    crowded = crowded | (flag_own[...] + flag_layer[...] > 2 * slots)
    flag_row_src[...] = jnp.where(crowded, 1, 0)
    f1 = [
        remote(flag_row_src, flag_row.at[o - 1], f1_send.at[o - 1], f1_recv.at[o - 1], at(o, 0))
        for o in range(1, n_row)
    ]
    to_smem.wait()
    load_a.wait()

    def blocks_of(step, r):
        q = 2 * lax.rem(r, half) + r // half
        return [table_s[step, 4 * q + k] for k in range(4)]

    def from_first(place):
        return b_first[jnp.where(place < first, place, first)]

    def from_all(place):
        last = jnp.where(place < first, capacity - first, place - first)
        return jnp.where(place < first, from_first(place), b_last[last])

    def product(a, block, r):
        left = jnp.concatenate([a[2 * r], a[2 * r + 1]], axis=1)
        right = jnp.concatenate(
            [jnp.concatenate(block[:2], axis=1), jnp.concatenate(block[2:], axis=1)], axis=0
        )
        return jnp.dot(left, right, preferred_element_type=jnp.float32)

    @pl.loop(0, rows, unroll=4)
    def _(r):
        part[r] = product(av, [bv[place] for place in blocks_of(0, r)], r)

    worst = flag_row_src[...]
    for o in range(1, n_row):
        f1[o - 1].wait()
        worst = jnp.maximum(worst, flag_row[o - 1])
    flag_col_src[...] = worst
    f2 = [
        remote(flag_col_src, flag_col.at[o - 1], f2_send.at[o - 1], f2_recv.at[o - 1], at(0, o))
        for o in range(1, n_col)
    ]
    for o in range(1, n_col):
        f2[o - 1].wait()
        worst = jnp.maximum(worst, flag_col[o - 1])
    flag_ref[...] = worst[0:1, 0:1]

    theirs = (1 - layer) * half
    mine = layer * half
    early = first // 8
    middle = (early + half + 1) // 2
    l_copies = []

    def add_step(base, low, high, read):
        @pl.loop(low, high, unroll=high - low)
        def _(k):
            r = base + k
            part[r] += product(a_in, [read(place) for place in blocks_of(1, r)], r)

    def hand_over(low, high):
        c = len(l_copies)
        l_copies.append(
            remote(
                part.at[pl.ds(theirs + low, high - low)], layer_in.at[pl.ds(low, high - low)],
                l_send.at[c], l_recv.at[c], at(0, 0, 1),
            )
        )

    ready = 2 if early <= rows // CHUNKS else CHUNKS
    for copy in a_copies[:ready] + b_copies[:2]:
        copy.wait_recv()
    add_step(theirs, 0, early, from_first)
    hand_over(0, early)
    add_step(mine, 0, early, from_first)

    if window:
        b_copies[2].wait_recv()
        back = remote(
            b_last.at[pl.ds(body - first, window)], b_last.at[pl.ds(slots - first, window)],
            e_send.at[1], e_recv.at[1], at(0, 0, 1),
        )
    for copy in a_copies[ready:] + b_copies[-1:]:
        copy.wait_recv()
    if window:
        back.wait_recv()
    add_step(theirs, early, middle, from_all)
    hand_over(early, middle)
    add_step(theirs, middle, half, from_all)
    hand_over(middle, half)
    add_step(mine, early, half, from_all)

    for copy, (low, high) in zip(l_copies, ((0, early), (early, middle), (middle, half))):
        copy.wait_recv()

        @pl.loop(low, high, unroll=high - low)
        def _(k):
            total = (part[mine + k] + layer_in[k]).astype(out_ref.dtype)
            out_ref[k, 0] = total[:, : out_ref.shape[3]]
            out_ref[k, 1] = total[:, out_ref.shape[3] :]

    shared = [handed, back] if window else []
    for copy in list(sends.values()) + a_copies + b_copies + shared + l_copies:
        copy.wait_send()


def call(n_row, n_col, slots, window, collective_id, a_cols, a_count, b_cols, b_count, c_cols, a, b):
    ka, rows = a_cols.shape
    kb, panel = b_cols.shape
    kc = c_cols.shape[0]
    size, width = a.shape[1], b.shape[2]
    half = rows // 2
    capacity = slots + window
    first = (slots - window) * 2 // 3 // 8 * 8
    vmem = pltpu.VMEM
    dma = pltpu.SemaphoreType.DMA
    tile = (8, LANES)
    in_hbm = pl.BlockSpec(memory_space=pltpu.HBM)
    in_vmem = pl.BlockSpec(memory_space=vmem)
    return pl.pallas_call(
        functools.partial(kernel, n_row, n_col, slots, window, first),
        out_shape=(
            jax.ShapeDtypeStruct((half, kc, size, width), jnp.bfloat16),
            jax.ShapeDtypeStruct((1, 1), jnp.int32),
        ),
        in_specs=[in_hbm] * 7,
        out_specs=(in_vmem, in_vmem),
        scratch_shapes=[
            vmem(a_cols.shape, jnp.int32),
            vmem(a_count.shape, jnp.int32),
            vmem(b_cols.shape, jnp.int32),
            vmem(b_count.shape, jnp.int32),
            vmem(c_cols.shape, jnp.int32),
            vmem(tile, jnp.int32),
            vmem(tile, jnp.int32),
            vmem((rows * ka, size, size), jnp.bfloat16),
            vmem((panel * kb + 1, size, width), jnp.bfloat16),
            vmem((rows * ka, size, size), jnp.bfloat16),
            vmem((first + 1, size, width), jnp.bfloat16),
            vmem((capacity - first + 1, size, width), jnp.bfloat16),
            vmem((slots, size, width), jnp.bfloat16),
            vmem((max(window, 1), size, width), jnp.bfloat16),
            vmem((max(window, 1), size, width), jnp.bfloat16),
            vmem((rows, size, kc * width), jnp.float32),
            vmem((half, size, kc * width), jnp.float32),
            vmem((4,) + tile, jnp.int32),
            vmem((2, LANES), jnp.int32),
            pltpu.SMEM((2, LANES), jnp.int32),
            vmem((1, LANES), jnp.int32),
            pltpu.SMEM((1, LANES), jnp.int32),
            vmem(tile, jnp.int32),
            vmem(tile, jnp.int32),
            vmem(tile, jnp.int32),
            vmem((n_row - 1,) + tile, jnp.int32),
            vmem(tile, jnp.int32),
            vmem((n_col - 1,) + tile, jnp.int32),
            dma((9,)),
            dma((4,)), dma((4,)),
            dma((CHUNKS,)), dma((CHUNKS,)),
            dma((CHUNKS,)), dma((CHUNKS,)),
            dma((2,)), dma((2,)),
            dma((3,)), dma((3,)),
            dma((1,)), dma((1,)),
            dma((n_row - 1,)), dma((n_row - 1,)),
            dma((n_col - 1,)), dma((n_col - 1,)),
        ],
        compiler_params=pltpu.CompilerParams(
            collective_id=collective_id, has_side_effects=True, vmem_limit_bytes=62 * 1024 * 1024
        ),
        cost_estimate=pl.CostEstimate(
            flops=4 * rows * size * ka * size * kc * width, bytes_accessed=6 << 20, transcendentals=0
        ),
    )(a_cols, a_count, b_cols, b_count, c_cols, a, b)


def local(n_row, n_col, a_blocks, a_cols, a_count, b_blocks, b_cols, b_count, c_cols):
    a_panel, b_panel = a_blocks[0, 0, 0], b_blocks[0, 0, 0]
    args = (
        a_cols[0, 0, 0].T, a_count[0, 0], b_cols[0, 0, 0].T, b_count[0, 0], c_cols[0, 0].T,
        a_panel.reshape((-1,) + a_panel.shape[2:]), b_panel.reshape((-1,) + b_panel.shape[2:]),
    )
    every = a_panel.shape[0] * a_panel.shape[1] * c_cols.shape[3]
    quick, over = call(n_row, n_col, SLOTS, WINDOW, 0, *args)
    result = lax.cond(
        over[0, 0] > 0,
        lambda args, quick: call(n_row, n_col, every, 0, 1, *args)[0],
        lambda args, quick: quick,
        args, quick,
    )
    return result[None, None]


def solution(mesh):
    return jax.shard_map(
        functools.partial(local, mesh.shape["row"], mesh.shape["col"]),
        mesh=mesh,
        in_specs=(
            P("row", "col", "layer", None, None, None, None),
            P("row", "col", "layer", None, None),
            P("row", "col", "layer", None),
            P("row", "col", "layer", None, None, None, None),
            P("row", "col", "layer", None, None),
            P("row", "col", "layer", None),
            P("row", "col", None, None),
        ),
        out_specs=P("row", "col", "layer", None, None, None),
        check_vma=False,
    )
```

```python
import functools

import jax
import jax.numpy as jnp
from jax import lax
from jax.experimental import pallas as pl
from jax.experimental.pallas import tpu as pltpu
from jax.sharding import PartitionSpec as P

SLOTS = 28
WINDOW = 4
CHUNKS = 4
ABSENT = 1000
LANES = 128


def block_row(lane, rows):
    q = lane // 4
    return (q % 2) * (rows // 2) + q // 2


def fill_lists(tile_ref, rows_ref, a_cols, a_count, b_cols, b_count, c_cols):
    ka, rows = a_cols.shape
    kc = c_cols.shape[0]
    kb, panel = b_cols.shape
    stride = panel // rows
    r = lax.broadcasted_iota(jnp.int32, (ka, rows), 1)
    t = lax.broadcasted_iota(jnp.int32, (ka, rows), 0)
    offset = a_cols[...] - stride * r + 1
    offset = jnp.where(offset < 0, offset + panel, offset)
    offset = jnp.where(offset >= panel, offset - panel, offset)
    u = lax.broadcasted_iota(jnp.int32, (kb, panel), 0)
    rows_ref[...] = jnp.full(rows_ref.shape, ABSENT, jnp.int32)
    rows_ref[0:ka, 0:rows] = jnp.where(t < a_count[...], offset, ABSENT)
    rows_ref[ka : ka + kc, 0:rows] = c_cols[...]
    rows_ref[ka + kc : ka + kc + kb, 0:panel] = jnp.where(u < b_count[...], b_cols[...], -1)
    columns = jnp.transpose(rows_ref[...])

    def along(height, source, column):
        place = lax.broadcasted_iota(jnp.int32, (height, LANES), 0)
        entries = jnp.broadcast_to(columns[:height, column : column + 1], (height, LANES))
        return jnp.sum(jnp.where(place == source(height), entries, 0), axis=0, keepdims=True)

    def own_row(height):
        return block_row(lax.broadcasted_iota(jnp.int32, (height, LANES), 1), rows)

    lane = lax.broadcasted_iota(jnp.int32, (1, LANES), 1)
    a_slots = [along(rows, own_row, k) for k in range(ka)]
    c_slots = [along(rows, own_row, ka + k) for k in range(kc)]
    tile_ref[0:1] = jnp.where(lane % 4 < 2, a_slots[0], a_slots[1])
    tile_ref[1:2] = jnp.where(lane % 2 == 0, c_slots[0], c_slots[1])
    for d in range(stride):

        def near(height):
            m = own_row(height) * stride + (d - 1)
            return jnp.where(m < 0, m + panel, m)

        for k in range(kb):
            row = 2 + d * kb + k
            tile_ref[row : row + 1] = along(panel, near, ka + kc + k)


def matched(a_row, c_row, b_rows, rows, panel, kb):
    shape = (8, LANES)
    stride = panel // rows
    lane = lax.broadcasted_iota(jnp.int32, shape, 1)
    r = block_row(lane, rows)
    a_row = jnp.broadcast_to(a_row, shape)
    c_row = jnp.broadcast_to(c_row, shape)
    need = jnp.zeros(shape, jnp.int32)
    place = jnp.full(shape, panel * kb, jnp.int32)
    for d in range(stride):
        m = r * stride + (d - 1)
        m = jnp.where(m < 0, m + panel, m)
        for u in range(kb):
            k = d * kb + u
            hit = (a_row == d) & (c_row == jnp.broadcast_to(b_rows[k : k + 1], shape))
            hit = hit & (lane < rows * 4)
            need = jnp.where(hit, 1, need)
            place = jnp.where(hit, m * kb + u, place)
    return need, place


def earlier(need):
    lane = lax.broadcasted_iota(jnp.int32, need.shape, 1)
    total = need
    step = 1
    while step < LANES:
        total = total + jnp.where(lane >= step, pltpu.roll(total, step, 1), 0)
        step *= 2
    return total - need


def kernel(
    n_row, n_col, slots, window, first,
    a_cols_hbm, a_count_hbm, b_cols_hbm, b_count_hbm, c_cols_hbm, a_hbm, b_hbm,
    out_ref, flag_ref,
    a_cols, a_count, b_cols, b_count, c_cols,
    lists_ref, rows_ref,
    av, bv, a_in, b_first, b_all, packed, extra, extra_in, part, layer_in, tiles, table_v, table_s, send_v, send_s,
    flag_own, flag_layer, flag_row_src, flag_row, flag_col_src, flag_col,
    local_sem, list_send, list_recv, a_send, a_recv, b_send, b_recv, e_send, e_recv, l_send, l_recv,
    f0_send, f0_recv, f1_send, f1_recv, f2_send, f2_recv,
):
    row = lax.axis_index("row")
    col = lax.axis_index("col")
    layer = lax.axis_index("layer")
    rows = out_ref.shape[0] * 2
    half = rows // 2
    kb, panel = b_cols.shape
    capacity = slots + window

    def at(d_row, d_col, d_layer=0):
        return {
            "row": lax.rem(row + d_row + n_row, n_row),
            "col": lax.rem(col + d_col + n_col, n_col),
            "layer": lax.rem(layer + d_layer, 2),
        }

    loads = [
        pltpu.make_async_copy(src, dst, local_sem.at[4 + k])
        for k, (src, dst) in enumerate((
            (a_cols_hbm, a_cols), (a_count_hbm, a_count), (b_cols_hbm, b_cols),
            (b_count_hbm, b_count), (c_cols_hbm, c_cols),
        ))
    ]
    for load in loads:
        load.start()

    barrier = pltpu.get_barrier_semaphore()
    partners = [at(o, 0) for o in range(1, n_row)] + [at(0, o) for o in range(1, n_col)]
    partners += [at(0, 0, 1), at(1, -1), at(-1, 1)]
    for partner in partners:
        pl.semaphore_signal(barrier, inc=1, device_id=partner, device_id_type=pl.DeviceIdType.MESH)

    zero = jnp.zeros(bv.shape[1:], bv.dtype)
    bv[panel * kb] = zero
    b_first[first] = zero
    b_all[capacity] = zero
    for load in loads:
        load.wait()
    load_b = pltpu.make_async_copy(b_hbm, bv.at[pl.ds(0, panel * kb)], local_sem.at[0])
    load_b.start()
    load_a = pltpu.make_async_copy(a_hbm, av, local_sem.at[1])
    load_a.start()
    fill_lists(lists_ref, rows_ref, a_cols, a_count, b_cols, b_count, c_cols)
    own = lists_ref[...]
    need, place = matched(own[0:1], own[1:2], own[2:], rows, panel, kb)
    table_v[0:1] = place[0:1]

    pl.semaphore_wait(barrier, len(partners))

    def remote(src, dst, send, recv, device):
        copy = pltpu.make_async_remote_copy(
            src_ref=src, dst_ref=dst, send_sem=send, recv_sem=recv,
            device_id=device, device_id_type=pl.DeviceIdType.MESH,
        )
        copy.start()
        return copy

    sends = {}
    for slot, device in ((2, at(1, 0)), (3, at(1, -1)), (1, at(-1, 0)), (0, at(0, -1))):
        sends[slot] = remote(lists_ref, tiles.at[slot], list_send.at[slot], list_recv.at[slot], device)
    a_copies = []
    a_per = av.shape[0] // CHUNKS
    for c in (0, CHUNKS // 2, 1, CHUNKS // 2 + 1):
        piece = pl.ds(c * a_per, a_per)
        a_copies.append(
            remote(a_hbm.at[piece], a_in.at[piece], a_send.at[c], a_recv.at[c], at(0, -1))
        )

    sends[2].wait_recv()
    sends[3].wait_recv()
    need, place = matched(tiles[3, 0:1], tiles[2, 1:2], own[2:], rows, panel, kb)
    spread = (rows * 4, LANES)
    lane = lax.broadcasted_iota(jnp.int32, spread, 1)
    entry = lax.broadcasted_iota(jnp.int32, spread, 0)
    needed = jnp.broadcast_to(need[0:1], spread)
    before = jnp.sum(jnp.where(lane < entry, needed, 0), axis=1, keepdims=True)
    taken = jnp.where(lane == entry, needed * (1 + jnp.broadcast_to(place[0:1], spread)), 0)
    taken = jnp.broadcast_to(jnp.sum(taken, axis=1, keepdims=True), spread)
    here = (jnp.broadcast_to(before, spread) == lane) & (taken > 0)
    count = jnp.sum(need, axis=1, keepdims=True)
    chosen = jnp.sum(jnp.where(here, taken - 1, 0), axis=0, keepdims=True)
    send_v[...] = jnp.where(lane[0:1] == LANES - 1, count[0:1], chosen)
    to_smem = pltpu.make_async_copy(send_v, send_s, local_sem.at[2])
    to_smem.start()
    flag_own[...] = jnp.broadcast_to(count, flag_own.shape)
    f0 = remote(flag_own, flag_layer, f0_send.at[0], f0_recv.at[0], at(0, 0, 1))
    load_b.wait()
    to_smem.wait()
    if window:
        for k in range(window):
            extra[k] = bv[send_s[0, slots + k]]
        handed = remote(extra, extra_in, e_send.at[0], e_recv.at[0], at(0, 0, 1))
    b_copies = []

    def send_b(low, high):
        c = len(b_copies)
        landing = (b_first if low < first else b_all).at[pl.ds(low, high - low)]
        b_copies.append(
            remote(packed.at[pl.ds(low, high - low)], landing, b_send.at[c], b_recv.at[c], at(-1, 0))
        )

    body = slots - window
    for low, high in ((0, first // 2), (first // 2, first)):
        for k in range(low, high):
            packed[k] = bv[send_s[0, k]]
        send_b(low, high)
    f0.wait()
    crowded = jnp.maximum(flag_own[...], flag_layer[...]) > capacity
    crowded = crowded | (flag_own[...] + flag_layer[...] > 2 * slots)
    flag_row_src[...] = jnp.where(crowded, 1, 0)
    f1 = [
        remote(flag_row_src, flag_row.at[o - 1], f1_send.at[o - 1], f1_recv.at[o - 1], at(o, 0))
        for o in range(1, n_row)
    ]
    if window:
        handed.wait_recv()
        for k in range(body, slots):
            packed[k] = jnp.where(k < send_s[0, LANES - 1], bv[send_s[0, k]], extra_in[slots - 1 - k])
        send_b(body, slots)
    for k in range(first, body):
        packed[k] = bv[send_s[0, k]]
    send_b(first, body)

    sends[0].wait_recv()
    sends[1].wait_recv()
    need, place = matched(tiles[0, 0:1], own[1:2], tiles[1][2:], rows, panel, kb)
    before = earlier(need)
    before = jnp.where((need > 0) & (before < capacity), before, capacity)
    back = (before >= slots) & (before < capacity)
    table_v[1:2] = jnp.where(back, slots + capacity - 1 - before, before)[0:1]
    to_smem = pltpu.make_async_copy(table_v, table_s, local_sem.at[3])
    to_smem.start()

    to_smem.wait()
    load_a.wait()

    def blocks_of(step, r):
        q = 2 * lax.rem(r, half) + r // half
        return [table_s[step, 4 * q + k] for k in range(4)]

    def from_first(place):
        return b_first[jnp.where(place < first, place, first)]

    def product(a, block, r):
        left = jnp.concatenate([a[2 * r], a[2 * r + 1]], axis=1)
        right = jnp.concatenate(
            [jnp.concatenate(block[:2], axis=1), jnp.concatenate(block[2:], axis=1)], axis=0
        )
        return jnp.dot(left, right, preferred_element_type=jnp.float32)

    @pl.loop(0, rows, unroll=4)
    def _(r):
        part[r] = product(av, [bv[place] for place in blocks_of(0, r)], r)

    theirs = (1 - layer) * half
    mine = layer * half
    early = first // 8
    middle = (early + half + 1) // 2
    l_copies = []

    def step_one(read, r):
        return part[r] + product(a_in, [read(place) for place in blocks_of(1, r)], r)

    def for_other(low, high, read):
        @pl.loop(low, high, unroll=high - low)
        def _(k):
            part[theirs + k] = step_one(read, theirs + k)

        hand_over(low, high)

    def for_result(low, high, read):
        @pl.loop(low, high, unroll=high - low)
        def _(k):
            total = (step_one(read, mine + k) + layer_in[k]).astype(out_ref.dtype)
            out_ref[k, 0] = total[:, : out_ref.shape[3]]
            out_ref[k, 1] = total[:, out_ref.shape[3] :]

    def hand_over(low, high):
        c = len(l_copies)
        l_copies.append(
            remote(
                part.at[pl.ds(theirs + low, high - low)], layer_in.at[pl.ds(low, high - low)],
                l_send.at[c], l_recv.at[c], at(0, 0, 1),
            )
        )

    ready = 2 if early <= rows // CHUNKS else CHUNKS
    for copy in a_copies[:ready] + b_copies[:2]:
        copy.wait_recv()
    for_other(0, early, from_first)

    worst = flag_row_src[...]
    for o in range(1, n_row):
        f1[o - 1].wait()
        worst = jnp.maximum(worst, flag_row[o - 1])
    flag_col_src[...] = worst
    f2 = [
        remote(flag_col_src, flag_col.at[o - 1], f2_send.at[o - 1], f2_recv.at[o - 1], at(0, o))
        for o in range(1, n_col)
    ]

    @pl.loop(0, first, unroll=4)
    def _(k):
        b_all[k] = b_first[k]

    l_copies[0].wait_recv()
    for_result(0, early, from_first)

    if window:
        b_copies[2].wait_recv()
        back = remote(
            b_all.at[pl.ds(body, window)], b_all.at[pl.ds(slots, window)],
            e_send.at[1], e_recv.at[1], at(0, 0, 1),
        )
    for copy in a_copies[ready:] + b_copies[-1:]:
        copy.wait_recv()
    if window:
        back.wait_recv()

    def from_all(place):
        return b_all[place]

    for_other(early, middle, from_all)
    for_other(middle, half, from_all)
    l_copies[1].wait_recv()
    for_result(early, middle, from_all)
    l_copies[2].wait_recv()
    for_result(middle, half, from_all)

    for o in range(1, n_col):
        f2[o - 1].wait()
        worst = jnp.maximum(worst, flag_col[o - 1])
    flag_ref[...] = worst[0:1, 0:1]

    shared = [handed, back] if window else []
    for copy in list(sends.values()) + a_copies + b_copies + shared + l_copies:
        copy.wait_send()


def call(n_row, n_col, slots, window, collective_id, a_cols, a_count, b_cols, b_count, c_cols, a, b):
    ka, rows = a_cols.shape
    kb, panel = b_cols.shape
    kc = c_cols.shape[0]
    size, width = a.shape[1], b.shape[2]
    half = rows // 2
    capacity = slots + window
    first = (slots - window) * 2 // 3 // 8 * 8
    vmem = pltpu.VMEM
    dma = pltpu.SemaphoreType.DMA
    tile = (8, LANES)
    in_hbm = pl.BlockSpec(memory_space=pltpu.HBM)
    in_vmem = pl.BlockSpec(memory_space=vmem)
    return pl.pallas_call(
        functools.partial(kernel, n_row, n_col, slots, window, first),
        out_shape=(
            jax.ShapeDtypeStruct((half, kc, size, width), jnp.bfloat16),
            jax.ShapeDtypeStruct((1, 1), jnp.int32),
        ),
        in_specs=[in_hbm] * 7,
        out_specs=(in_vmem, in_vmem),
        scratch_shapes=[
            vmem(a_cols.shape, jnp.int32),
            vmem(a_count.shape, jnp.int32),
            vmem(b_cols.shape, jnp.int32),
            vmem(b_count.shape, jnp.int32),
            vmem(c_cols.shape, jnp.int32),
            vmem(tile, jnp.int32),
            vmem(tile, jnp.int32),
            vmem((rows * ka, size, size), jnp.bfloat16),
            vmem((panel * kb + 1, size, width), jnp.bfloat16),
            vmem((rows * ka, size, size), jnp.bfloat16),
            vmem((first + 1, size, width), jnp.bfloat16),
            vmem((capacity + 1, size, width), jnp.bfloat16),
            vmem((slots, size, width), jnp.bfloat16),
            vmem((max(window, 1), size, width), jnp.bfloat16),
            vmem((max(window, 1), size, width), jnp.bfloat16),
            vmem((rows, size, kc * width), jnp.float32),
            vmem((half, size, kc * width), jnp.float32),
            vmem((4,) + tile, jnp.int32),
            vmem((2, LANES), jnp.int32),
            pltpu.SMEM((2, LANES), jnp.int32),
            vmem((1, LANES), jnp.int32),
            pltpu.SMEM((1, LANES), jnp.int32),
            vmem(tile, jnp.int32),
            vmem(tile, jnp.int32),
            vmem(tile, jnp.int32),
            vmem((n_row - 1,) + tile, jnp.int32),
            vmem(tile, jnp.int32),
            vmem((n_col - 1,) + tile, jnp.int32),
            dma((9,)),
            dma((4,)), dma((4,)),
            dma((CHUNKS,)), dma((CHUNKS,)),
            dma((CHUNKS,)), dma((CHUNKS,)),
            dma((2,)), dma((2,)),
            dma((3,)), dma((3,)),
            dma((1,)), dma((1,)),
            dma((n_row - 1,)), dma((n_row - 1,)),
            dma((n_col - 1,)), dma((n_col - 1,)),
        ],
        compiler_params=pltpu.CompilerParams(
            collective_id=collective_id, has_side_effects=True, vmem_limit_bytes=62 * 1024 * 1024
        ),
        cost_estimate=pl.CostEstimate(
            flops=4 * rows * size * ka * size * kc * width, bytes_accessed=6 << 20, transcendentals=0
        ),
    )(a_cols, a_count, b_cols, b_count, c_cols, a, b)


def local(n_row, n_col, a_blocks, a_cols, a_count, b_blocks, b_cols, b_count, c_cols):
    a_panel, b_panel = a_blocks[0, 0, 0], b_blocks[0, 0, 0]
    args = (
        a_cols[0, 0, 0].T, a_count[0, 0], b_cols[0, 0, 0].T, b_count[0, 0], c_cols[0, 0].T,
        a_panel.reshape((-1,) + a_panel.shape[2:]), b_panel.reshape((-1,) + b_panel.shape[2:]),
    )
    every = a_panel.shape[0] * a_panel.shape[1] * c_cols.shape[3]
    quick, over = call(n_row, n_col, SLOTS, WINDOW, 0, *args)
    result = lax.cond(
        over[0, 0] > 0,
        lambda args, quick: call(n_row, n_col, every, 0, 1, *args)[0],
        lambda args, quick: quick,
        args, quick,
    )
    return result[None, None]


def solution(mesh):
    return jax.shard_map(
        functools.partial(local, mesh.shape["row"], mesh.shape["col"]),
        mesh=mesh,
        in_specs=(
            P("row", "col", "layer", None, None, None, None),
            P("row", "col", "layer", None, None),
            P("row", "col", "layer", None),
            P("row", "col", "layer", None, None, None, None),
            P("row", "col", "layer", None, None),
            P("row", "col", "layer", None),
            P("row", "col", None, None),
        ),
        out_specs=P("row", "col", "layer", None, None, None),
        check_vma=False,
    )
```

```python
import functools

import jax
import jax.numpy as jnp
from jax import lax
from jax.experimental import pallas as pl
from jax.experimental.pallas import tpu as pltpu
from jax.sharding import PartitionSpec as P

SLOTS = 28
WINDOW = 4
FIRST = 20
EARLY = 4
CHUNKS = 4
ABSENT = 1000
LANES = 128


def block_row(lane, rows):
    q = lane // 4
    return (q % 2) * (rows // 2) + q // 2


def fill_lists(tile_ref, rows_ref, a_cols, a_count, b_cols, b_count, c_cols):
    ka, rows = a_cols.shape
    kc = c_cols.shape[0]
    kb, panel = b_cols.shape
    stride = panel // rows
    r = lax.broadcasted_iota(jnp.int32, (ka, rows), 1)
    t = lax.broadcasted_iota(jnp.int32, (ka, rows), 0)
    offset = a_cols[...] - stride * r + 1
    offset = jnp.where(offset < 0, offset + panel, offset)
    offset = jnp.where(offset >= panel, offset - panel, offset)
    u = lax.broadcasted_iota(jnp.int32, (kb, panel), 0)
    rows_ref[...] = jnp.full(rows_ref.shape, ABSENT, jnp.int32)
    rows_ref[0:ka, 0:rows] = jnp.where(t < a_count[...], offset, ABSENT)
    rows_ref[ka : ka + kc, 0:rows] = c_cols[...]
    rows_ref[ka + kc : ka + kc + kb, 0:panel] = jnp.where(u < b_count[...], b_cols[...], -1)
    columns = jnp.transpose(rows_ref[...])

    def along(height, source, column):
        place = lax.broadcasted_iota(jnp.int32, (height, LANES), 0)
        entries = jnp.broadcast_to(columns[:height, column : column + 1], (height, LANES))
        return jnp.sum(jnp.where(place == source(height), entries, 0), axis=0, keepdims=True)

    def own_row(height):
        return block_row(lax.broadcasted_iota(jnp.int32, (height, LANES), 1), rows)

    lane = lax.broadcasted_iota(jnp.int32, (1, LANES), 1)
    a_slots = [along(rows, own_row, k) for k in range(ka)]
    c_slots = [along(rows, own_row, ka + k) for k in range(kc)]
    tile_ref[0:1] = jnp.where(lane % 4 < 2, a_slots[0], a_slots[1])
    tile_ref[1:2] = jnp.where(lane % 2 == 0, c_slots[0], c_slots[1])
    for d in range(stride):

        def near(height):
            m = own_row(height) * stride + (d - 1)
            return jnp.where(m < 0, m + panel, m)

        for k in range(kb):
            row = 2 + d * kb + k
            tile_ref[row : row + 1] = along(panel, near, ka + kc + k)


def matched(a_row, c_row, b_rows, rows, panel, kb):
    shape = (8, LANES)
    stride = panel // rows
    lane = lax.broadcasted_iota(jnp.int32, shape, 1)
    r = block_row(lane, rows)
    a_row = jnp.broadcast_to(a_row, shape)
    c_row = jnp.broadcast_to(c_row, shape)
    need = jnp.zeros(shape, jnp.int32)
    place = jnp.full(shape, panel * kb, jnp.int32)
    for d in range(stride):
        m = r * stride + (d - 1)
        m = jnp.where(m < 0, m + panel, m)
        for u in range(kb):
            k = d * kb + u
            hit = (a_row == d) & (c_row == jnp.broadcast_to(b_rows[k : k + 1], shape))
            hit = hit & (lane < rows * 4)
            need = jnp.where(hit, 1, need)
            place = jnp.where(hit, m * kb + u, place)
    return need, place


def earlier(need):
    lane = lax.broadcasted_iota(jnp.int32, need.shape, 1)
    total = need
    step = 1
    while step < LANES:
        total = total + jnp.where(lane >= step, pltpu.roll(total, step, 1), 0)
        step *= 2
    return total - need


def kernel(
    n_row, n_col, slots, window, first, early,
    a_cols_hbm, a_count_hbm, b_cols_hbm, b_count_hbm, c_cols_hbm, a_hbm, b_hbm,
    out_ref, flag_ref,
    a_cols, a_count, b_cols, b_count, c_cols,
    lists_ref, rows_ref,
    av, bv, a_in, b_first, b_all, packed, extra, extra_in, part, layer_in, tiles, table_v, table_s, send_v, send_s,
    flag_own, flag_layer, flag_row_src, flag_row, flag_col_src, flag_col,
    local_sem, list_send, list_recv, a_send, a_recv, b_send, b_recv, e_send, e_recv, l_send, l_recv,
    f0_send, f0_recv, f1_send, f1_recv, f2_send, f2_recv,
):
    row = lax.axis_index("row")
    col = lax.axis_index("col")
    layer = lax.axis_index("layer")
    rows = out_ref.shape[0] * 2
    half = rows // 2
    kb, panel = b_cols.shape
    capacity = slots + window

    def at(d_row, d_col, d_layer=0):
        return {
            "row": lax.rem(row + d_row + n_row, n_row),
            "col": lax.rem(col + d_col + n_col, n_col),
            "layer": lax.rem(layer + d_layer, 2),
        }

    loads = [
        pltpu.make_async_copy(src, dst, local_sem.at[4 + k])
        for k, (src, dst) in enumerate((
            (a_cols_hbm, a_cols), (a_count_hbm, a_count), (b_cols_hbm, b_cols),
            (b_count_hbm, b_count), (c_cols_hbm, c_cols),
        ))
    ]
    for load in loads:
        load.start()

    barrier = pltpu.get_barrier_semaphore()
    partners = [at(o, 0) for o in range(1, n_row)] + [at(0, o) for o in range(1, n_col)]
    partners += [at(0, 0, 1), at(1, -1), at(-1, 1)]
    for partner in partners:
        pl.semaphore_signal(barrier, inc=1, device_id=partner, device_id_type=pl.DeviceIdType.MESH)

    zero = jnp.zeros(bv.shape[1:], bv.dtype)
    bv[panel * kb] = zero
    b_first[first] = zero
    b_all[capacity] = zero
    for load in loads:
        load.wait()
    load_b = pltpu.make_async_copy(b_hbm, bv.at[pl.ds(0, panel * kb)], local_sem.at[0])
    load_b.start()
    load_a = pltpu.make_async_copy(a_hbm, av, local_sem.at[1])
    load_a.start()
    fill_lists(lists_ref, rows_ref, a_cols, a_count, b_cols, b_count, c_cols)
    own = lists_ref[...]
    need, place = matched(own[0:1], own[1:2], own[2:], rows, panel, kb)
    table_v[0:1] = place[0:1]

    pl.semaphore_wait(barrier, len(partners))

    def remote(src, dst, send, recv, device):
        copy = pltpu.make_async_remote_copy(
            src_ref=src, dst_ref=dst, send_sem=send, recv_sem=recv,
            device_id=device, device_id_type=pl.DeviceIdType.MESH,
        )
        copy.start()
        return copy

    sends = {}
    for slot, device in ((2, at(1, 0)), (3, at(1, -1)), (1, at(-1, 0)), (0, at(0, -1))):
        sends[slot] = remote(lists_ref, tiles.at[slot], list_send.at[slot], list_recv.at[slot], device)
    a_copies = []
    a_per = av.shape[0] // CHUNKS
    for c in (0, CHUNKS // 2, 1, CHUNKS // 2 + 1):
        piece = pl.ds(c * a_per, a_per)
        a_copies.append(
            remote(a_hbm.at[piece], a_in.at[piece], a_send.at[c], a_recv.at[c], at(0, -1))
        )

    sends[2].wait_recv()
    sends[3].wait_recv()
    need, place = matched(tiles[3, 0:1], tiles[2, 1:2], own[2:], rows, panel, kb)
    spread = (rows * 4, LANES)
    lane = lax.broadcasted_iota(jnp.int32, spread, 1)
    entry = lax.broadcasted_iota(jnp.int32, spread, 0)
    needed = jnp.broadcast_to(need[0:1], spread)
    before = jnp.sum(jnp.where(lane < entry, needed, 0), axis=1, keepdims=True)
    taken = jnp.where(lane == entry, needed * (1 + jnp.broadcast_to(place[0:1], spread)), 0)
    taken = jnp.broadcast_to(jnp.sum(taken, axis=1, keepdims=True), spread)
    here = (jnp.broadcast_to(before, spread) == lane) & (taken > 0)
    count = jnp.sum(need, axis=1, keepdims=True)
    chosen = jnp.sum(jnp.where(here, taken - 1, 0), axis=0, keepdims=True)
    send_v[...] = jnp.where(lane[0:1] == LANES - 1, count[0:1], chosen)
    to_smem = pltpu.make_async_copy(send_v, send_s, local_sem.at[2])
    to_smem.start()
    soon = jnp.where(lax.broadcasted_iota(jnp.int32, need.shape, 1) < 8 * early, need, 0)
    soon = jnp.sum(soon, axis=1, keepdims=True)
    flag_own[...] = jnp.broadcast_to(jnp.where(soon > first, ABSENT, count), flag_own.shape)
    f0 = remote(flag_own, flag_layer, f0_send.at[0], f0_recv.at[0], at(0, 0, 1))
    load_b.wait()
    to_smem.wait()
    if window:
        for k in range(window):
            extra[k] = bv[send_s[0, slots + k]]
        handed = remote(extra, extra_in, e_send.at[0], e_recv.at[0], at(0, 0, 1))
    b_copies = []

    def send_b(low, high):
        c = len(b_copies)
        landing = (b_first if low < first else b_all).at[pl.ds(low, high - low)]
        b_copies.append(
            remote(packed.at[pl.ds(low, high - low)], landing, b_send.at[c], b_recv.at[c], at(-1, 0))
        )

    body = slots - window
    for low, high in ((0, first // 2), (first // 2, first)):
        for k in range(low, high):
            packed[k] = bv[send_s[0, k]]
        send_b(low, high)
    f0.wait()
    crowded = jnp.maximum(flag_own[...], flag_layer[...]) > capacity
    crowded = crowded | (flag_own[...] + flag_layer[...] > 2 * slots)
    flag_row_src[...] = jnp.where(crowded, 1, 0)
    f1 = [
        remote(flag_row_src, flag_row.at[o - 1], f1_send.at[o - 1], f1_recv.at[o - 1], at(o, 0))
        for o in range(1, n_row)
    ]
    if window:
        handed.wait_recv()
        for k in range(body, slots):
            packed[k] = jnp.where(k < send_s[0, LANES - 1], bv[send_s[0, k]], extra_in[slots - 1 - k])
        send_b(body, slots)
    for k in range(first, body):
        packed[k] = bv[send_s[0, k]]
    send_b(first, body)

    sends[0].wait_recv()
    sends[1].wait_recv()
    need, place = matched(tiles[0, 0:1], own[1:2], tiles[1][2:], rows, panel, kb)
    before = earlier(need)
    before = jnp.where((need > 0) & (before < capacity), before, capacity)
    back = (before >= slots) & (before < capacity)
    table_v[1:2] = jnp.where(back, slots + capacity - 1 - before, before)[0:1]
    to_smem = pltpu.make_async_copy(table_v, table_s, local_sem.at[3])
    to_smem.start()

    to_smem.wait()
    load_a.wait()

    def blocks_of(step, r):
        q = 2 * lax.rem(r, half) + r // half
        return [table_s[step, 4 * q + k] for k in range(4)]

    def from_first(place):
        return b_first[jnp.where(place < first, place, first)]

    def product(a, block, r):
        left = jnp.concatenate([a[2 * r], a[2 * r + 1]], axis=1)
        right = jnp.concatenate(
            [jnp.concatenate(block[:2], axis=1), jnp.concatenate(block[2:], axis=1)], axis=0
        )
        return jnp.dot(left, right, preferred_element_type=jnp.float32)

    @pl.loop(0, rows, unroll=4)
    def _(r):
        part[r] = product(av, [bv[place] for place in blocks_of(0, r)], r)

    theirs = (1 - layer) * half
    mine = layer * half
    middle = (early + half + 1) // 2
    l_copies = []

    def step_one(read, r):
        return part[r] + product(a_in, [read(place) for place in blocks_of(1, r)], r)

    def for_other(low, high, read):
        @pl.loop(low, high, unroll=high - low)
        def _(k):
            part[theirs + k] = step_one(read, theirs + k)

        hand_over(low, high)

    def for_result(low, high, read):
        @pl.loop(low, high, unroll=high - low)
        def _(k):
            total = (step_one(read, mine + k) + layer_in[k]).astype(out_ref.dtype)
            out_ref[k, 0] = total[:, : out_ref.shape[3]]
            out_ref[k, 1] = total[:, out_ref.shape[3] :]

    def hand_over(low, high):
        c = len(l_copies)
        l_copies.append(
            remote(
                part.at[pl.ds(theirs + low, high - low)], layer_in.at[pl.ds(low, high - low)],
                l_send.at[c], l_recv.at[c], at(0, 0, 1),
            )
        )

    ready = 2 if early <= rows // CHUNKS else CHUNKS
    for copy in a_copies[:ready] + b_copies[:2]:
        copy.wait_recv()
    for_other(0, early, from_first)

    worst = flag_row_src[...]
    for o in range(1, n_row):
        f1[o - 1].wait()
        worst = jnp.maximum(worst, flag_row[o - 1])
    flag_col_src[...] = worst
    f2 = [
        remote(flag_col_src, flag_col.at[o - 1], f2_send.at[o - 1], f2_recv.at[o - 1], at(0, o))
        for o in range(1, n_col)
    ]

    @pl.loop(0, first, unroll=4)
    def _(k):
        b_all[k] = b_first[k]

    l_copies[0].wait_recv()
    for_result(0, early, from_first)

    if window:
        b_copies[2].wait_recv()
        back = remote(
            b_all.at[pl.ds(body, window)], b_all.at[pl.ds(slots, window)],
            e_send.at[1], e_recv.at[1], at(0, 0, 1),
        )
    for copy in a_copies[ready:] + b_copies[-1:]:
        copy.wait_recv()
    if window:
        back.wait_recv()

    def from_all(place):
        return b_all[place]

    for_other(early, middle, from_all)
    for_other(middle, half, from_all)
    l_copies[1].wait_recv()
    for_result(early, middle, from_all)
    l_copies[2].wait_recv()
    for_result(middle, half, from_all)

    for o in range(1, n_col):
        f2[o - 1].wait()
        worst = jnp.maximum(worst, flag_col[o - 1])
    flag_ref[...] = worst[0:1, 0:1]

    shared = [handed, back] if window else []
    for copy in list(sends.values()) + a_copies + b_copies + shared + l_copies:
        copy.wait_send()


def call(n_row, n_col, slots, window, first, early, collective_id, a_cols, a_count, b_cols, b_count, c_cols, a, b):
    ka, rows = a_cols.shape
    kb, panel = b_cols.shape
    kc = c_cols.shape[0]
    size, width = a.shape[1], b.shape[2]
    half = rows // 2
    capacity = slots + window
    vmem = pltpu.VMEM
    dma = pltpu.SemaphoreType.DMA
    tile = (8, LANES)
    in_hbm = pl.BlockSpec(memory_space=pltpu.HBM)
    in_vmem = pl.BlockSpec(memory_space=vmem)
    return pl.pallas_call(
        functools.partial(kernel, n_row, n_col, slots, window, first, early),
        out_shape=(
            jax.ShapeDtypeStruct((half, kc, size, width), jnp.bfloat16),
            jax.ShapeDtypeStruct((1, 1), jnp.int32),
        ),
        in_specs=[in_hbm] * 7,
        out_specs=(in_vmem, in_vmem),
        scratch_shapes=[
            vmem(a_cols.shape, jnp.int32),
            vmem(a_count.shape, jnp.int32),
            vmem(b_cols.shape, jnp.int32),
            vmem(b_count.shape, jnp.int32),
            vmem(c_cols.shape, jnp.int32),
            vmem(tile, jnp.int32),
            vmem(tile, jnp.int32),
            vmem((rows * ka, size, size), jnp.bfloat16),
            vmem((panel * kb + 1, size, width), jnp.bfloat16),
            vmem((rows * ka, size, size), jnp.bfloat16),
            vmem((first + 1, size, width), jnp.bfloat16),
            vmem((capacity + 1, size, width), jnp.bfloat16),
            vmem((slots, size, width), jnp.bfloat16),
            vmem((max(window, 1), size, width), jnp.bfloat16),
            vmem((max(window, 1), size, width), jnp.bfloat16),
            vmem((rows, size, kc * width), jnp.float32),
            vmem((half, size, kc * width), jnp.float32),
            vmem((4,) + tile, jnp.int32),
            vmem((2, LANES), jnp.int32),
            pltpu.SMEM((2, LANES), jnp.int32),
            vmem((1, LANES), jnp.int32),
            pltpu.SMEM((1, LANES), jnp.int32),
            vmem(tile, jnp.int32),
            vmem(tile, jnp.int32),
            vmem(tile, jnp.int32),
            vmem((n_row - 1,) + tile, jnp.int32),
            vmem(tile, jnp.int32),
            vmem((n_col - 1,) + tile, jnp.int32),
            dma((9,)),
            dma((4,)), dma((4,)),
            dma((CHUNKS,)), dma((CHUNKS,)),
            dma((CHUNKS,)), dma((CHUNKS,)),
            dma((2,)), dma((2,)),
            dma((3,)), dma((3,)),
            dma((1,)), dma((1,)),
            dma((n_row - 1,)), dma((n_row - 1,)),
            dma((n_col - 1,)), dma((n_col - 1,)),
        ],
        compiler_params=pltpu.CompilerParams(
            collective_id=collective_id, has_side_effects=True, vmem_limit_bytes=62 * 1024 * 1024
        ),
        cost_estimate=pl.CostEstimate(
            flops=4 * rows * size * ka * size * kc * width, bytes_accessed=6 << 20, transcendentals=0
        ),
    )(a_cols, a_count, b_cols, b_count, c_cols, a, b)


def local(n_row, n_col, a_blocks, a_cols, a_count, b_blocks, b_cols, b_count, c_cols):
    a_panel, b_panel = a_blocks[0, 0, 0], b_blocks[0, 0, 0]
    args = (
        a_cols[0, 0, 0].T, a_count[0, 0], b_cols[0, 0, 0].T, b_count[0, 0], c_cols[0, 0].T,
        a_panel.reshape((-1,) + a_panel.shape[2:]), b_panel.reshape((-1,) + b_panel.shape[2:]),
    )
    every = a_panel.shape[0] * a_panel.shape[1] * c_cols.shape[3]
    quick, over = call(n_row, n_col, SLOTS, WINDOW, FIRST, EARLY, 0, *args)
    result = lax.cond(
        over[0, 0] > 0,
        lambda args, quick: call(n_row, n_col, every, 0, every // 2, every // 16, 1, *args)[0],
        lambda args, quick: quick,
        args, quick,
    )
    return result[None, None]


def solution(mesh):
    return jax.shard_map(
        functools.partial(local, mesh.shape["row"], mesh.shape["col"]),
        mesh=mesh,
        in_specs=(
            P("row", "col", "layer", None, None, None, None),
            P("row", "col", "layer", None, None),
            P("row", "col", "layer", None),
            P("row", "col", "layer", None, None, None, None),
            P("row", "col", "layer", None, None),
            P("row", "col", "layer", None),
            P("row", "col", None, None),
        ),
        out_specs=P("row", "col", "layer", None, None, None),
        check_vma=False,
    )
```
